128 devices in a mesh: attn: 8 (over z, core), expert: 16 (over x, y).
Axes of the slice: x: 4, y: 4, z: 4, core: 2. Of those that a mesh axis runs over, the one named last changes fastest.
Arguments:
- queries: bfloat16 [32, 64, 576], P('attn'), may hold values from -11 to 11
- cache: bfloat16 [24576, 64, 576], P(('attn', 'expert')), may hold values from -6 to 6
- owner: int32 [24576], P(('attn', 'expert')), may hold values from 0 to 4, as said below
- uv_weight: bfloat16 [64, 512, 128], P('expert'), may hold values from -0.25 to 0.25
- out_weight: bfloat16 [8192, 7168], P('expert')
- norm_gain: float32 [7168], replicated, may hold values from 0.1 to 1.9
- expert_ids: int32 [32, 8], P('attn'), may hold values from 0 to 15, all different within a row; in each aligned block of 4 rows (0 to 3, 4 to 7, ...) at most 4 rows name the same one
- gate_values: float32 [32, 8], P('attn'), may hold values from 0.1 to 1
- gate_weight: bfloat16 [16, 7168, 2048], P('attn', None, 'expert'), may hold values from -0.0625 to 0.0625
- up_weight: bfloat16 [16, 7168, 2048], P('attn', None, 'expert'), may hold values from -0.0625 to 0.0625
- down_weight: bfloat16 [16, 2048, 7168], P('attn', 'expert'), may hold values from -0.1875 to 0.1875
Outputs:
- layer_out: bfloat16 [32, 7168], P('attn', 'expert')
The draws below stay inside these ranges and needn't reach their ends.
Inputs may be any that keep to these rules, and one draw needn't show every extreme that they name: owner[p] names one of the 4 requests of page p's attention index, or is 4 for an empty slot; every request holds at least one page. `expert_ids`: among the rows of one attention index, no expert is named by more than 4 rows.
All inputs are finite; a program needn't handle non-finite values.
Results may differ from the reference program's by a relative error of at most 0.035.
Values may be sent and summed in bfloat16 or wider, within the bound.
A program may use at most 192 MiB of HBM per device.

```python
import math
import jax
import jax.numpy as jnp
import numpy as np
from jax import lax

D = 7168
FF = 2048
HEADS = 64
LATENT = 512
VDIM = 128
PAGE = 64
TOP = 8
ROWS_A = 4
POOL = 192
KDIM = 576
ROWS = 32
EXPERTS = 16
CAP = 4
PAGES = 24576
N_ATTN = 8
N_EXPERT = 16


def special_tokens(key):
    return jax.random.normal(jax.random.fold_in(key, 101), (N_ATTN, ROWS_A, 2, KDIM), jnp.float32)


def draw_cache(key, part):
    specials = special_tokens(key)
    key = jax.random.fold_in(key, 7)
    baseline = jnp.clip(jax.random.normal(key, (PAGES, PAGE, KDIM), jnp.float32), -6.0, 6.0)
    page_number = jnp.arange(PAGES, dtype=jnp.int32)
    group_index = page_number // (N_EXPERT * POOL)
    device_column = page_number // POOL % N_EXPERT
    request = page_number % POOL * N_EXPERT + device_column
    marked = (request < ROWS_A) & (request % 4 == 0)
    safe_request = jnp.minimum(request, ROWS_A - 1)
    replaced = specials[group_index, safe_request]
    leading = jnp.where(marked[:, None, None], replaced, baseline[:, :2])
    return jnp.concatenate([leading, baseline[:, 2:]], axis=1).astype(jnp.bfloat16)


def draw_queries(key, part):
    key = jax.random.fold_in(key, 3)
    drawn = jnp.clip(jax.random.normal(key, (ROWS, HEADS, KDIM), jnp.float32) * 0.8, -6.0, 6.0)
    return drawn.astype(jnp.bfloat16)


def draw_owner(key, part):
    key = jax.random.fold_in(key, 11)
    subkeys = jax.random.split(key, 5)
    device_count = N_ATTN * N_EXPERT
    device_index = jnp.arange(device_count, dtype=jnp.int32)
    column = device_index % N_EXPERT
    group_index = device_index // N_EXPERT
    filled = jax.random.randint(subkeys[0], (device_count,), POOL // 2, POOL)
    full_column = jax.random.randint(subkeys[1], (N_ATTN,), 0, N_EXPERT)
    filled = jnp.where(column == full_column[group_index], POOL, filled)
    slot_number = jnp.arange(POOL, dtype=jnp.int32)
    forced = slot_number[None, :] * N_EXPERT + column[:, None]
    grid_shape = (device_count, POOL)
    skewed = jnp.minimum(jax.random.randint(subkeys[2], grid_shape, 0, ROWS_A), jax.random.randint(subkeys[3], grid_shape, 0, ROWS_A))
    skewed = jnp.minimum(skewed, jax.random.randint(subkeys[4], grid_shape, 0, ROWS_A))
    chosen = jnp.where(forced < ROWS_A, forced, skewed)
    owners = jnp.where(slot_number[None, :] < filled[:, None], chosen, ROWS_A)
    return owners.reshape(-1).astype(jnp.int32)


def draw_out_weight(key, part):
    key = jax.random.fold_in(key, 5)
    subkeys = jax.random.split(key, 2)
    baseline = jax.random.normal(subkeys[0], (HEADS * VDIM, D), jnp.float32) * (HEADS * VDIM) ** (-0.5)
    column_scale = jnp.exp(jax.random.uniform(subkeys[1], (1, D), jnp.float32) * math.log(10.0)) / 12.0
    return (baseline * column_scale).astype(jnp.bfloat16)


def spiked(array, rng, source, target, shards_of, factor):
    def block_of(axis_at):
        return (jnp.arange(array.shape[axis_at]) // (array.shape[axis_at] // shards_of)).reshape((-1,) + (1,) * (array.ndim - 1 - axis_at))

    near = jax.random.permutation(rng, shards_of)[block_of(target)]
    far = (block_of(target) + shards_of // 2) % shards_of
    return jnp.where((block_of(source) == near) | (block_of(source) == far), factor * array, array)


def level_of(key, shape, cuts, smallest, high):
    factor_of = 1.0
    for axis_at, shards_of in cuts:
        draws = jax.random.uniform(jax.random.fold_in(jax.random.fold_in(key, 6), axis_at), (shards_of,), jnp.float32, smallest / len(cuts), high / len(cuts))
        factor_of = factor_of * jnp.repeat(jnp.exp(draws), shape[axis_at] // shards_of).reshape((-1,) + (1,) * (len(shape) - 1 - axis_at))
    return factor_of


def routed_block(rng, own, number, rows, amount, top, most, skew):
    ranking = jax.random.permutation(rng, amount)
    packed, usual = shares(amount, rows * top, most, skew, True), shares(amount, rows * top, most, skew, False)
    places = jnp.arange(amount)

    def named(lengths, offset_by):
        used = int((lengths > 0).sum())
        fixed = max(1, used // 4)
        passed = fixed + (places - fixed + offset_by * (used - fixed)) % max(1, amount - fixed)
        return jnp.zeros((amount,), jnp.int32).at[ranking[jnp.where(places < fixed, places, passed)]].set(jnp.asarray(lengths, jnp.int32))

    lengths = jnp.where(number % 4 == 0, named(packed, number // 4), named(usual, number - number // 4 - 1))
    mixed = jax.random.permutation(jax.random.fold_in(own, 3), amount)
    giver, sink = mixed[0:amount // 2 * 2:2], mixed[1:amount // 2 * 2:2]
    slack = jnp.minimum(lengths[giver] - 1, most - lengths[sink]) // 2
    slack = jnp.where((giver == ranking[0]) | (sink == ranking[0]) | (lengths[sink] == 0), 0, jnp.maximum(slack, 0))
    passed = jax.random.randint(jax.random.fold_in(own, 4), (amount // 2,), 0, 1 << 20) % (slack + 1)
    lengths = lengths.at[giver].add(-passed).at[sink].add(passed)
    items = jnp.searchsorted(jnp.cumsum(lengths), jnp.arange(rows * top), side="right").astype(jnp.int32)
    table = items.reshape(top, rows).T
    table = table[jax.random.permutation(jax.random.fold_in(own, 1), rows)]
    offset_by = jax.random.randint(jax.random.fold_in(own, 2), (rows, 1), 0, top)
    return jnp.take_along_axis(table, (jnp.arange(top)[None, :] + offset_by) % top, axis=1)


def shares(number_of, total, most, slope, full):
    weights = [(1 << 20) // math.isqrt(standing ** slope) + 1 for standing in range(1, number_of + 1)]
    largest = most if full else min(most, max(-(-total // number_of), total * weights[0] // sum(weights)))
    least = 1 if total - largest >= number_of - 1 else 0
    counts, spare = [largest] + [least] * (number_of - 1), total - largest - least * (number_of - 1)
    while spare > 0:
        free = [i for i in range(1, number_of) if counts[i] < largest] or [i for i in range(1, number_of) if counts[i] < most]
        whole, remaining = sum([weights[i] for i in free]), spare
        for i in free:
            extra = min(most - counts[i], max(1, remaining * weights[i] // whole), spare)
            counts[i] = counts[i] + extra
            spare = spare - extra
    return np.array(counts)


def centred(rng, shape, deviation, most, pieces=(), kind=jnp.bfloat16):
    gain = level_of(rng, shape, pieces, -0.22, 0.18) if pieces else 1.0
    array = jax.random.normal(rng, shape, jnp.float32) * deviation * gain
    return jnp.minimum(jnp.maximum(array, -most), most).astype(kind)


def noise_with(stream_key, dims, deviation, limit, shards, heavy, kind=jnp.bfloat16):
    values = deviation * jax.random.normal(stream_key, dims, jnp.float32)
    if shards:
        values = values * level_of(stream_key, dims, shards, -0.22, 0.18)
    return jnp.clip(spiked(values, jax.random.fold_in(stream_key, 3), *heavy), -limit, limit).astype(kind)


def setup_inputs(seed: int = 0) -> dict:
    key_of = jax.random.split(jax.random.key(seed), 12)
    queries = draw_queries(jax.random.fold_in(key_of[11], 71), 0)
    cache = draw_cache(jax.random.fold_in(key_of[11], 71), 0)
    owner = draw_owner(jax.random.fold_in(key_of[11], 71), 0)
    uv_weight = centred(key_of[3], (HEADS, LATENT, VDIM), LATENT ** -0.5, 0.25, ((0, 16),))
    out_weight = draw_out_weight(jax.random.fold_in(key_of[11], 71), 0)
    norm_gain = jnp.clip(1.0 + 0.18 * jax.random.normal(key_of[5], (D,), jnp.float32), 0.1, 1.9)
    expert_ids_keys = jax.random.split(jax.random.fold_in(key_of[6], 1), ROWS // ROWS_A)
    expert_ids_turns = jax.random.permutation(jax.random.fold_in(key_of[6], 3), ROWS // ROWS_A)
    expert_ids = jax.vmap(lambda own, number: routed_block(jax.random.fold_in(key_of[6], 2), own, number, ROWS_A, EXPERTS, TOP, CAP, 2))(expert_ids_keys, expert_ids_turns).reshape((ROWS, TOP))
    gate_values = jnp.clip(jnp.exp(math.log(1.0) - 2.3025851 * jax.random.uniform(key_of[7], (ROWS, TOP), jnp.float32) ** level_of(key_of[7], (ROWS, TOP), ((0, 8),), -0.2, 0.2)), 0.1, 1.0)
    gate_weight = centred(key_of[8], (EXPERTS, D, FF), D ** -0.5, 0.0625, ((0, 8), (2, 16)))
    up_weight = centred(key_of[9], (EXPERTS, D, FF), D ** -0.5, 0.0625, ((0, 8), (2, 16)))
    down_weight = noise_with(key_of[10], (EXPERTS, FF, D), FF ** -0.5, 0.1875, ((0, 8), (1, 16)), (1, 2, 16, 2.0))
    return dict(queries=queries, cache=cache, owner=owner, uv_weight=uv_weight, out_weight=out_weight, norm_gain=norm_gain, expert_ids=expert_ids, gate_values=gate_values, gate_weight=gate_weight, up_weight=up_weight, down_weight=down_weight)


NEGATIVE = -1e+30
SCORE_SCALE = 192.0 ** (-0.5)
EPSILON = 1e-06
HIGHEST = lax.Precision.HIGHEST

def group_attention(operands):
    group_queries, group_pages, group_owner = operands
    row_count = group_queries.shape[0]
    valid_pages = group_owner < row_count
    safe_owner = jnp.minimum(group_owner, row_count - 1)
    picked = jnp.take(group_queries, safe_owner, axis=0).astype(jnp.float32)
    scores = jnp.einsum('phc,ptc->pht', picked, group_pages.astype(jnp.float32), precision=HIGHEST) * SCORE_SCALE
    page_max = jnp.where(valid_pages[:, None], lax.optimization_barrier(jnp.max(scores, axis=2)), NEGATIVE)
    member = (safe_owner[:, None] == jnp.arange(row_count, dtype=jnp.int32)[None, :]) & valid_pages[:, None]
    row_max = lax.optimization_barrier(jnp.max(jnp.where(member[:, :, None], page_max[:, None, :], NEGATIVE), axis=0))
    weights = jnp.where(valid_pages[:, None, None], jnp.exp(scores - jnp.take(row_max, safe_owner, axis=0)[:, :, None]), 0.0)
    probs = weights.astype(jnp.bfloat16).astype(jnp.float32)
    page_sum = jnp.einsum('pht,ptc->phc', probs, group_pages[:, :, :LATENT].astype(jnp.float32), precision=HIGHEST)
    member_float = member.astype(jnp.float32)
    totals = jnp.dot(member_float.T, lax.optimization_barrier(jnp.sum(weights, axis=2)), precision=HIGHEST)
    summed = jnp.dot(member_float.T, page_sum.reshape(page_sum.shape[0], -1), precision=HIGHEST)
    return summed.reshape(row_count, HEADS, LATENT) / totals[:, :, None]

def reference(queries, cache, owner, uv_weight, out_weight, norm_gain, expert_ids, gate_values, gate_weight, up_weight, down_weight):
    grouped = (queries.reshape(N_ATTN, ROWS_A, HEADS, KDIM), cache.reshape(N_ATTN, N_EXPERT * POOL, PAGE, KDIM), owner.reshape(N_ATTN, N_EXPERT * POOL))
    attended = lax.map(group_attention, grouped).reshape(ROWS, HEADS, LATENT).astype(jnp.bfloat16)
    mixed_heads = jnp.einsum('rhc,hcv->rhv', attended.astype(jnp.float32), uv_weight.astype(jnp.float32), precision=HIGHEST)
    mixed_heads = mixed_heads.astype(jnp.bfloat16).reshape(ROWS, HEADS * VDIM)
    attn_out = jnp.dot(mixed_heads, out_weight, preferred_element_type=jnp.float32)
    mean_square = lax.optimization_barrier(jnp.mean(attn_out * attn_out, axis=1, keepdims=True))
    normed = (attn_out * lax.rsqrt(mean_square + EPSILON) * norm_gain[None, :]).astype(jnp.bfloat16)
    routing = lax.optimization_barrier(jnp.sum(jnp.where(expert_ids[:, :, None] == jnp.arange(EXPERTS, dtype=jnp.int32)[None, None, :], gate_values[:, :, None], 0.0), axis=1))

    def one_expert(running, expert_index):
        gate_proj = jnp.dot(normed, gate_weight[expert_index], preferred_element_type=jnp.float32)
        up_proj = jnp.dot(normed, up_weight[expert_index], preferred_element_type=jnp.float32)
        hidden = (jax.nn.silu(gate_proj) * up_proj).astype(jnp.bfloat16)
        produced = jnp.dot(hidden, down_weight[expert_index], preferred_element_type=jnp.float32)
        column = lax.dynamic_slice_in_dim(routing, expert_index, 1, 1)
        return (running + column * produced, None)
    expert_sum, unused = lax.scan(one_expert, jnp.zeros((ROWS, D), jnp.float32), jnp.arange(EXPERTS, dtype=jnp.int32))
    return (attn_out + expert_sum).astype(jnp.bfloat16)
```

```python
import functools
import jax
import jax.numpy as jnp
from jax import lax
from jax.experimental import pallas as pl
from jax.experimental.pallas import tpu as pltpu
from jax.sharding import PartitionSpec as P

SCORE_SCALE = 192.0 ** (-0.5)
LOG2E = 1.4426950408889634
EPSILON = 1e-06
MASKED = -1e30
FLOOR = -1e20
F32 = jnp.float32
BF16 = jnp.bfloat16
MESH = pl.DeviceIdType.MESH

NE = 16
CHUNK_PAGES = 16


def split_bf16(value, parts):
    out = []
    for _ in range(parts):
        piece = value.astype(BF16).astype(F32)
        out.append(piece)
        value = value - piece
    return out


def attention_kernel(owner, q_ref, cache_ref, out_ref, q_rows, m_ref, l_ref, acc_ref):
    step = pl.program_id(0)
    rows = 256
    tokens = CHUNK_PAGES * 64

    @pl.when(step == 0)
    def _():
        i = lax.broadcasted_iota(jnp.int32, (rows, rows), 0)
        j = lax.broadcasted_iota(jnp.int32, (rows, rows), 1)
        order = (j == (i % 4) * 64 + i // 4).astype(F32).astype(BF16)
        q_rows[...] = jnp.dot(
            order, q_ref[...].reshape(rows, 576), preferred_element_type=F32
        ).astype(BF16)
        m_ref[...] = jnp.full_like(m_ref, FLOOR)
        l_ref[...] = jnp.zeros_like(l_ref)
        acc_ref[...] = jnp.zeros_like(acc_ref)

    lane = lax.broadcasted_iota(jnp.int32, (8, 128), 1)
    request = lax.broadcasted_iota(jnp.int32, (8, 128), 0) % 4
    bias = []
    for pair in range(CHUNK_PAGES // 2):
        first = owner[step * CHUNK_PAGES + 2 * pair]
        second = owner[step * CHUNK_PAGES + 2 * pair + 1]
        bias.append(jnp.where(jnp.where(lane < 64, first, second) == request, 0.0, MASKED))
    bias = jnp.concatenate(bias, axis=1)
    keys = cache_ref[...].reshape(tokens, 576)
    scores = lax.dot_general(
        q_rows[...], keys, (((1,), (1,)), ((), ())), preferred_element_type=F32
    )
    scores = scores.reshape(32, 8, tokens) * (SCORE_SCALE * LOG2E) + bias[None]
    scores = scores.reshape(rows, tokens)
    m_old = m_ref[...]
    m_new = jnp.maximum(m_old, jnp.max(scores, axis=1, keepdims=True))
    alpha = jnp.exp2(m_old - m_new)
    probs = jnp.exp2(scores - m_new[:, :1])
    l_ref[...] = l_ref[...] * alpha + jnp.sum(probs, axis=1, keepdims=True)
    m_ref[...] = m_new
    acc_ref[...] = acc_ref[...] * alpha[:, :1] + jnp.dot(
        probs.astype(BF16), keys[:, :512], preferred_element_type=F32
    )

    @pl.when(step == pl.num_programs(0) - 1)
    def _():
        total = l_ref[...]
        safe = jnp.where(total > 0.0, total, 1.0)
        lse = jnp.where(total > 0.0, m_ref[...] + jnp.log2(safe), FLOOR)
        wide = lax.broadcasted_iota(jnp.int32, (rows, 128), 1)
        pieces = split_bf16(lse, 3)
        coded = jnp.zeros((rows, 128), F32)
        for at, piece in enumerate(pieces):
            coded = jnp.where(wide == at, piece, coded)
        value = (acc_ref[...] / safe[:, :1]).astype(BF16)
        out_ref[:, :, :512] = value.reshape(16, 16, 512)
        out_ref[:, :, 512:] = coded.astype(BF16).reshape(16, 16, 128)


def attention(owner, queries, cache):
    pages = cache.shape[0]
    return pl.pallas_call(
        attention_kernel,
        out_shape=jax.ShapeDtypeStruct((16, 16, 640), BF16),
        grid_spec=pltpu.PrefetchScalarGridSpec(
            num_scalar_prefetch=1,
            grid=(pages // CHUNK_PAGES,),
            in_specs=[
                pl.BlockSpec((4, 64, 576), lambda i, o: (0, 0, 0)),
                pl.BlockSpec((CHUNK_PAGES, 64, 576), lambda i, o: (i, 0, 0)),
            ],
            out_specs=pl.BlockSpec((16, 16, 640), lambda i, o: (0, 0, 0)),
            scratch_shapes=[
                pltpu.VMEM((256, 576), BF16),
                pltpu.VMEM((256, 128), F32),
                pltpu.VMEM((256, 128), F32),
                pltpu.VMEM((256, 512), F32),
            ],
        ),
        compiler_params=pltpu.CompilerParams(vmem_limit_bytes=32 << 20),
        name="attention",
    )(owner, queries, cache)


def window_tile(e):
    return (e // 2) * 7 + (e % 2) * 3


def fold(rows4):
    return jnp.concatenate([rows4[:, 128 * j : 128 * j + 128] for j in range(4)], axis=0)


def layer_kernel(
    partial_hbm, uv_hbm, outw_hbm, gain_hbm, ids_ref, values_ref, gate_hbm, up_hbm, down_hbm,
    out_ref,
    uv, outw, gain, gate, up, down,
    part_recv, term_send, term_recv, z_send, z_recv, x_mine, x_buf,
    pair_send, pair_keep, pair_recv, plane_send, plane_recv, last_send, last_recv,
    load_sem, s1, r1, s2, r2, s3, r3, s4, r4, s5, r5, s6, r6, s7, r7, s8, r8,
):
    a = lax.axis_index("attn")
    e = lax.axis_index("expert")
    z = a // 2
    core = a % 2
    odd = e % 2
    sibling = {"attn": z * 2 + (1 - core)}

    def plane_peer(k):
        return lax.rem(e + k, NE)

    def z_peer(k):
        return lax.rem(z + k, 4)

    def remote(src, dst, send, recv, device):
        return pltpu.make_async_remote_copy(
            src_ref=src, dst_ref=dst, send_sem=send, recv_sem=recv,
            device_id=device, device_id_type=MESH,
        )

    loads = [
        pltpu.make_async_copy(src, dst, load_sem.at[n])
        for n, (src, dst) in enumerate(
            [(partial_hbm.at[e], part_recv.at[15]), (uv_hbm, uv), (outw_hbm, outw), (gain_hbm, gain),
             (gate_hbm, gate), (up_hbm, up), (down_hbm, down)]
        )
    ]
    for load in loads:
        load.start()

    barrier = pltpu.get_barrier_semaphore()
    for k in range(1, NE):
        pl.semaphore_signal(barrier, inc=1, device_id={"expert": plane_peer(k)}, device_id_type=MESH)
    for k in range(1, 4):
        pl.semaphore_signal(barrier, inc=1, device_id={"attn": z_peer(k) * 2 + core}, device_id_type=MESH)
    pl.semaphore_signal(barrier, inc=1, device_id=sibling, device_id_type=MESH)
    pl.semaphore_wait(barrier, 19)

    sends = []
    first = []
    for k in range(1, NE):
        to = plane_peer(k)
        copy = remote(partial_hbm.at[to], part_recv.at[k - 1], s1.at[k - 1], r1.at[k - 1], {"expert": to})
        copy.start()
        first.append(copy)
    sends += first

    lane = lax.broadcasted_iota(jnp.int32, (16, 128), 1)
    row = lax.broadcasted_iota(jnp.int32, (16, 128), 0)
    spot = lane % 64
    ids = jnp.concatenate([ids_ref[...]] * 4, axis=0)
    values = jnp.concatenate([values_ref[...]] * 4, axis=0)
    expert_at = jnp.where(spot < 32, spot - 16, spot - 32)
    expert_at = jnp.where((spot >= 16) & (spot < 48), expert_at, -1)
    routing = jnp.zeros((16, 128), F32)
    for k in range(8):
        routing += jnp.where(ids[:, k : k + 1] == expert_at, values[:, k : k + 1], 0.0)
    high, low = split_bf16(routing, 2)
    coded = jnp.where(spot < 32, high, low)
    side = (row // 4 == 3 * (1 - odd)) & (lane // 64 == 1 - odd)

    loads[0].wait()
    for copy in first:
        copy.wait_recv()

    lse = [jnp.sum(part_recv[s, :, 512:].astype(F32), axis=1, keepdims=True) for s in range(NE)]
    peak = functools.reduce(jnp.maximum, lse)
    total = jnp.zeros_like(peak)
    summed = jnp.zeros((16, 512), F32)
    for s in range(NE):
        weight = jnp.exp2(lse[s] - peak)
        total += weight
        summed += weight * part_recv[s, :, :512].astype(F32)
    attended = (summed / total).astype(BF16)
    loads[1].wait()
    mixed = []
    for h in range(4):
        mapped = jnp.dot(attended, uv[h], preferred_element_type=F32)
        mixed.append(jnp.concatenate([mapped[4 * h : 4 * h + 4]] * 4, axis=0))
    mixed = jnp.concatenate(mixed, axis=1).astype(BF16)
    loads[2].wait()

    def terms(to):
        start = pl.multiple_of(window_tile(to) * 128, 128)
        wide = jnp.dot(mixed, outw[:, pl.ds(start, 512)], preferred_element_type=F32)
        folded = jnp.zeros((16, 128), F32)
        for j in range(4):
            folded = jnp.where(row // 4 == j, wide[:, 128 * j : 128 * j + 128], folded)
        return folded

    second = []
    for k in range(1, NE):
        to = plane_peer(k)
        term_send[k - 1] = terms(to).astype(BF16)
        copy = remote(term_send.at[k - 1], term_recv.at[k - 1], s2.at[k - 1], r2.at[k - 1], {"expert": to})
        copy.start()
        second.append(copy)
    sends += second
    attn_out = terms(e)
    for copy in second:
        copy.wait_recv()
    for k in range(NE - 1):
        attn_out += term_recv[k].astype(F32)

    loads[3].wait()
    gains = gain[pl.ds(window_tile(e), 4), :]
    gains = jnp.concatenate([jnp.broadcast_to(gains[j : j + 1], (4, 128)) for j in range(4)], axis=0)
    squares = jnp.sum(jnp.where(side, 0.0, attn_out * attn_out), axis=1, keepdims=True)
    squares = squares[0:4] + squares[4:8] + squares[8:12] + squares[12:16]
    squares = jnp.broadcast_to(jnp.concatenate([squares] * 4, axis=0), (16, 128))
    high, low = split_bf16(squares, 2)
    coded = jnp.where(spot == 0, high, jnp.where(spot == 1, low, coded))
    mine = jnp.where(side, coded, attn_out * gains).astype(BF16)
    z_send[...] = mine
    third = []
    for k in range(1, 4):
        copy = remote(z_send, z_recv.at[z], s3.at[k - 1], r3.at[z], {"attn": z_peer(k) * 2 + core})
        copy.start()
        third.append(copy)
    sends += third
    z_recv[z] = mine
    for k in range(1, 4):
        remote(z_send, z_recv.at[z_peer(k)], s3.at[k - 1], r3.at[z_peer(k)], sibling).wait_recv()
    blocks = [z_recv[n].astype(F32) for n in range(4)]
    wide = jnp.concatenate(
        [jnp.concatenate([blocks[n][4 * j : 4 * j + 4] for n in range(4)], axis=0) for j in range(4)],
        axis=1,
    )
    x_mine[...] = wide.astype(BF16)
    x_buf[e, core] = wide.astype(BF16)
    for k in range(1, NE):
        to = plane_peer(k)
        copy = remote(x_mine, x_buf.at[e, core], s4.at[k - 1], r4.at[e], {"expert": to})
        copy.start()
        sends.append(copy)
    copy = remote(x_mine, x_buf.at[e, core], s5.at[0], r5.at[e], sibling)
    copy.start()
    sends.append(copy)
    for k in range(1, NE):
        source = plane_peer(k)
        block = x_buf.at[source, core]
        remote(x_mine, block, s4.at[k - 1], r4.at[source], sibling).wait_recv()
        copy = remote(block, block, s5.at[k], r5.at[source], sibling)
        copy.start()
        sends.append(copy)

    for load in loads[4:6]:
        load.wait()
    products = [jnp.zeros((32, 256), F32) for _ in range(2)]
    squares = jnp.zeros((32, 1), F32)
    lane32 = lax.broadcasted_iota(jnp.int32, (32, 128), 1)
    for k in range(8):
        pair = lax.rem(e // 2 + k, 8)
        for half in range(2):
            source = pair * 2 + half
            block = x_buf.at[source, 1 - core]
            remote(x_mine, block, s5.at[0], r5.at[source], sibling).wait_recv()
        even = x_buf[pair * 2].reshape(32, 512)
        odds = x_buf[pair * 2 + 1].reshape(32, 512)
        middle = jnp.where(lane32 < 64, even[:, 384:], odds[:, :128])
        extra = jnp.where(lane32 < 64, odds[:, :128], even[:, 384:])
        squares += jnp.sum(jnp.where(lane32 % 64 < 2, extra.astype(F32), 0.0), axis=1, keepdims=True)
        x = jnp.concatenate([even[:, :384], middle, odds[:, 128:]], axis=1)
        at = pl.ds(pl.multiple_of(pair * 896, 128), 896)
        for j in range(2):
            weights = jnp.concatenate([gate[j, at, :], up[j, at, :]], axis=1)
            products[j] += jnp.dot(x, weights, preferred_element_type=F32)
        if k == 0:
            base = jnp.where(odd == 1, 0, 64)
            share = []
            for j in range(2):
                number = 2 * a + j
                chosen = (lane32 == base + 16 + number) | (lane32 == base + 32 + number)
                share.append(jnp.sum(jnp.where(chosen, extra.astype(F32), 0.0), axis=1, keepdims=True))
    scale = lax.rsqrt(squares / 7168.0 + EPSILON)
    hidden = []
    for j in range(2):
        g = products[j][:, :128] * scale
        u = products[j][:, 128:] * scale
        hidden.append(g / (1.0 + jnp.exp(-g)) * u * share[j])
    hidden = jnp.concatenate(hidden, axis=1).astype(BF16)

    loads[6].wait()
    swap = []
    for k in range(8):
        pair = lax.rem(e // 2 + k, 8)
        at = pl.ds(pl.multiple_of(pair * 896, 128), 896)
        produced = jnp.dot(hidden, down[:, at], preferred_element_type=F32)
        top, bottom = produced[:16], produced[16:]
        pair_keep[k] = jnp.where(core == 0, top, bottom)
        pair_send[k] = jnp.where(core == 0, bottom, top).astype(BF16)
        copy = remote(pair_send.at[k], pair_recv.at[k], s6.at[k], r6.at[k], sibling)
        copy.start()
        swap.append(copy)
    sends += swap
    seventh = []
    for k in range(8):
        pair = lax.rem(e // 2 + k, 8)
        swap[k].wait_recv()
        both = pair_keep[k] + pair_recv[k].astype(F32)
        lower, upper = both[:, :512], both[:, 384:]
        if k == 0:
            own = jnp.where(odd == 1, upper, lower)
            plane_send[0] = jnp.where(odd == 1, lower, upper).astype(BF16)
            targets = [(0, pair * 2 + (1 - odd))]
        else:
            plane_send[2 * k - 1] = lower.astype(BF16)
            plane_send[2 * k] = upper.astype(BF16)
            targets = [(2 * k - 1, pair * 2), (2 * k, pair * 2 + 1)]
        for at, to in targets:
            slot = lax.rem(e - to + NE, NE) - 1
            copy = remote(plane_send.at[at], plane_recv.at[slot], s7.at[at], r7.at[slot], {"expert": to})
            copy.start()
            sends.append(copy)
    for k in range(NE - 1):
        remote(plane_send.at[0], plane_recv.at[k], s7.at[0], r7.at[k], sibling).wait_recv()
        own += plane_recv[k].astype(F32)

    for n in range(4):
        last_send[n] = fold(own[4 * n : 4 * n + 4]).astype(BF16)
    last = []
    for k in range(1, 4):
        to = z_peer(k)
        copy = remote(last_send.at[to], last_recv.at[k - 1], s8.at[k - 1], r8.at[k - 1], {"attn": to * 2 + core})
        copy.start()
        last.append(copy)
    sends += last
    result = attn_out + last_send[z].astype(F32)
    for copy in last:
        copy.wait_recv()
    for k in range(3):
        result += last_recv[k].astype(F32)
    out_ref[...] = jnp.concatenate([result[4 * j : 4 * j + 4] for j in range(4)], axis=1).astype(BF16)
    for copy in sends:
        copy.wait_send()


def layer(partial, uv, outw, gain, ids, values, gate, up, down):
    dma = pltpu.SemaphoreType.DMA
    hbm = pl.BlockSpec(memory_space=pl.ANY)
    vmem = pl.BlockSpec(memory_space=pltpu.VMEM)
    return pl.pallas_call(
        layer_kernel,
        out_shape=jax.ShapeDtypeStruct((4, 512), BF16),
        in_specs=[hbm, hbm, hbm, hbm, vmem, vmem, hbm, hbm, hbm],
        out_specs=vmem,
        scratch_shapes=[
            pltpu.VMEM(uv.shape, BF16),
            pltpu.VMEM(outw.shape, BF16),
            pltpu.VMEM(gain.shape, F32),
            pltpu.VMEM(gate.shape, BF16),
            pltpu.VMEM(up.shape, BF16),
            pltpu.VMEM(down.shape, BF16),
            pltpu.VMEM((16, 16, 640), BF16),
            pltpu.VMEM((15, 16, 128), BF16),
            pltpu.VMEM((15, 16, 128), BF16),
            pltpu.VMEM((16, 128), BF16),
            pltpu.VMEM((4, 16, 128), BF16),
            pltpu.VMEM((16, 512), BF16),
            pltpu.VMEM((16, 2, 16, 512), BF16),
            pltpu.VMEM((8, 16, 896), BF16),
            pltpu.VMEM((8, 16, 896), F32),
            pltpu.VMEM((8, 16, 896), BF16),
            pltpu.VMEM((15, 16, 512), BF16),
            pltpu.VMEM((15, 16, 512), BF16),
            pltpu.VMEM((4, 16, 128), BF16),
            pltpu.VMEM((3, 16, 128), BF16),
            dma((7,)),
            dma((15,)), dma((15,)),
            dma((15,)), dma((15,)),
            dma((3,)), dma((4,)),
            dma((15,)), dma((16,)),
            dma((16,)), dma((16,)),
            dma((8,)), dma((8,)),
            dma((15,)), dma((15,)),
            dma((3,)), dma((3,)),
        ],
        compiler_params=pltpu.CompilerParams(
            collective_id=0, has_side_effects=True, vmem_limit_bytes=48 << 20
        ),
        name="layer",
    )(partial, uv, outw, gain, ids, values, gate, up, down)


def on_device(
    queries, cache, owner, uv_weight, out_weight, norm_gain, expert_ids, gate_values,
    gate_weight, up_weight, down_weight,
):
    partial = attention(owner, queries, cache)
    wide = layer(
        partial, uv_weight, out_weight, norm_gain.reshape(56, 128), expert_ids, gate_values,
        gate_weight, up_weight, down_weight.reshape(256, 7168),
    )
    start = (lax.axis_index("expert") % 2) * 64
    return lax.dynamic_slice_in_dim(wide, start, 448, 1)


def solution(mesh):
    placed = (
        P("attn", None, None),
        P(("attn", "expert"), None, None),
        P(("attn", "expert")),
        P("expert", None, None),
        P("expert", None),
        P(),
        P("attn", None),
        P("attn", None),
        P("attn", None, "expert"),
        P("attn", None, "expert"),
        P("attn", "expert", None),
    )
    return jax.shard_map(
        on_device, mesh=mesh, in_specs=placed, out_specs=P("attn", "expert"), check_vma=False
    )
```

```python
import functools
import jax
import jax.numpy as jnp
from jax import lax
from jax.experimental import pallas as pl
from jax.experimental.pallas import tpu as pltpu
from jax.sharding import PartitionSpec as P

SCORE_SCALE = 192.0 ** (-0.5)
LOG2E = 1.4426950408889634
EPSILON = 1e-06
MASKED = -1e30
FLOOR = -1e20
F32 = jnp.float32
BF16 = jnp.bfloat16
MESH = pl.DeviceIdType.MESH

NX = 4
PAGES = 192
STEP_PAGES = 32
LOAD_PAGES = 16
START_WEIGHTS = 3


def hops(steps):
    return sum(min(d, NX - d) for d in steps)


OFFSETS = sorted(
    [(z, x, y) for z in range(NX) for x in range(NX) for y in range(NX) if (z, x, y) != (0, 0, 0)],
    key=lambda d: -hops(d),
)
PLANE = [d[1:] for d in OFFSETS if d[0] == 0]
PAIRS = [(0, 0), (0, 1), (1, 0), (3, 0), (1, 1), (3, 1), (2, 0), (2, 1)]


def split_bf16(value, parts):
    out = []
    for _ in range(parts):
        piece = value.astype(BF16).astype(F32)
        out.append(piece)
        value = value - piece
    return out


def window_tile(e):
    return (e // 2) * 7 + (e % 2) * 3


def layer_kernel(
    queries_hbm, cache_hbm, owner_hbm, uv_hbm, outw_hbm, gain_hbm, ids_hbm, values_hbm, gate_hbm, up_hbm, down_hbm,
    out_ref,
    owner, queries, q_rows, cache, scores, peak_ref, total_ref, value_ref,
    uv, outw, gain, ids_ref, values_ref, gate, up, down,
    part_send, part_recv, term_send, term_recv, x_mine, x_buf,
    swap_send, swap_keep, swap_recv, back_send, back_recv,
    load_sem, cache_sem, s1, r1, s2, r2, s3, r3, s4, r4, s5, r5, s6, r6, s7, r7, s8, r8,
):
    a = lax.axis_index("attn")
    e = lax.axis_index("expert")
    z = a // 2
    core = a % 2
    ex = e // NX
    ey = e % NX
    odd = e % 2
    sibling = {"attn": z * 2 + (1 - core)}

    def plane_peer(x, y):
        return lax.rem(ex + x, NX) * NX + lax.rem(ey + y, NX)

    def z_peer(k):
        return lax.rem(z + k, NX)

    def device(k, x, y):
        return {"attn": z_peer(k) * 2 + core, "expert": plane_peer(x, y)}

    def remote(src, dst, send, recv, to):
        return pltpu.make_async_remote_copy(
            src_ref=src, dst_ref=dst, send_sem=send, recv_sem=recv, device_id=to, device_id_type=MESH
        )

    owner_load = pltpu.make_async_copy(owner_hbm, owner, load_sem.at[0])
    queries_load = pltpu.make_async_copy(queries_hbm, queries, load_sem.at[1])
    owner_load.start()
    queries_load.start()
    cache_loads = []
    for c in range(PAGES // LOAD_PAGES):
        at = pl.ds(c * LOAD_PAGES, LOAD_PAGES)
        cache_loads.append(pltpu.make_async_copy(cache_hbm.at[at], cache.at[at], cache_sem.at[c]))
        cache_loads[-1].start()
    loads = [
        pltpu.make_async_copy(src, dst, load_sem.at[n + 2])
        for n, (src, dst) in enumerate(
            [(uv_hbm, uv), (outw_hbm, outw), (gain_hbm, gain), (ids_hbm, ids_ref), (values_hbm, values_ref),
             (gate_hbm, gate), (up_hbm, up), (down_hbm, down)]
        )
    ]
    barrier = pltpu.get_barrier_semaphore()
    for offset in OFFSETS:
        pl.semaphore_signal(barrier, inc=1, device_id=device(*offset), device_id_type=MESH)
    pl.semaphore_signal(barrier, inc=1, device_id=sibling, device_id_type=MESH)

    owner_load.wait()
    queries_load.wait()
    rows = 256
    i = lax.broadcasted_iota(jnp.int32, (rows, rows), 0)
    j = lax.broadcasted_iota(jnp.int32, (rows, rows), 1)
    order = (j == (i % 4) * 64 + i // 4).astype(F32).astype(BF16)
    q_rows[...] = jnp.dot(order, queries[...].reshape(rows, 576), preferred_element_type=F32).astype(BF16)
    lane8 = lax.broadcasted_iota(jnp.int32, (8, 128), 1)
    request = lax.broadcasted_iota(jnp.int32, (8, 128), 0) % 4
    tokens = STEP_PAGES * 64
    steps = PAGES // STEP_PAGES
    per = STEP_PAGES // LOAD_PAGES
    peak_ref[...] = jnp.full((rows, 128), FLOOR, F32)
    for c in range(steps):
        for load in cache_loads[c * per : (c + 1) * per]:
            load.wait()
        if c == START_WEIGHTS:
            for load in loads:
                load.start()
        keys = cache[c * STEP_PAGES : (c + 1) * STEP_PAGES].reshape(tokens, 576)
        raw = lax.dot_general(q_rows[...], keys, (((1,), (1,)), ((), ())), preferred_element_type=F32)
        peak = peak_ref[...]
        for pair in range(STEP_PAGES // 2):
            first = owner[c * STEP_PAGES + 2 * pair]
            second = owner[c * STEP_PAGES + 2 * pair + 1]
            bias = jnp.where(jnp.where(lane8 < 64, first, second) == request, 0.0, MASKED)
            tile = raw[:, 128 * pair : 128 * pair + 128].reshape(32, 8, 128) * (SCORE_SCALE * LOG2E) + bias[None]
            tile = tile.reshape(rows, 128)
            scores[c, :, 128 * pair : 128 * pair + 128] = tile
            peak = jnp.maximum(peak, tile)
        peak_ref[...] = peak
    peak = jnp.max(peak_ref[...], axis=1, keepdims=True)
    peak_ref[...] = jnp.broadcast_to(peak, (rows, 128))
    total_ref[...] = jnp.zeros((rows, 128), F32)
    value_ref[...] = jnp.zeros((rows, 512), F32)

    def weigh(c, carry):
        peak = peak_ref[...]
        total = total_ref[...]
        probs = []
        for pair in range(STEP_PAGES // 2):
            prob = jnp.exp2(scores[c, :, 128 * pair : 128 * pair + 128] - peak)
            total = total + prob
            probs.append(prob.astype(BF16))
        total_ref[...] = total
        values = cache[pl.ds(c * STEP_PAGES, STEP_PAGES), :, :512].reshape(tokens, 512)
        value_ref[...] += jnp.dot(jnp.concatenate(probs, axis=1), values, preferred_element_type=F32)
        return carry

    lax.fori_loop(0, steps, weigh, 0)
    total = jnp.sum(total_ref[...], axis=1, keepdims=True)
    safe = jnp.where(total > 0.0, total, 1.0)
    lse = jnp.where(total > 0.0, peak_ref[...] + jnp.log2(safe), FLOOR)
    wide = lax.broadcasted_iota(jnp.int32, (rows, 128), 1)
    coded = jnp.zeros((rows, 128), F32)
    for at, piece in enumerate(split_bf16(lse, 3)):
        coded = jnp.where(wide == at, piece, coded)
    part_send[:, :, :512] = (value_ref[...] / safe).astype(BF16).reshape(16, 16, 512)
    part_send[:, :, 512:] = coded.astype(BF16).reshape(16, 16, 128)

    pl.semaphore_wait(barrier, len(OFFSETS) + 1)
    sends = []
    first = []
    for k, offset in enumerate(PLANE):
        to = plane_peer(*offset)
        first.append(remote(part_send.at[to], part_recv.at[k], s1.at[k], r1.at[k], {"expert": to}))
        first[-1].start()
    sends += first

    for load in loads[:5]:
        load.wait()
    lane = lax.broadcasted_iota(jnp.int32, (16, 128), 1)
    row = lax.broadcasted_iota(jnp.int32, (16, 128), 0)
    spot = lane % 64
    ids = jnp.concatenate([ids_ref[...]] * 4, axis=0)
    shares = jnp.concatenate([values_ref[...]] * 4, axis=0)
    expert_at = jnp.where(spot < 32, spot - 16, spot - 32)
    expert_at = jnp.where((spot >= 16) & (spot < 48), expert_at, -1)
    routing = jnp.zeros((16, 128), F32)
    for k in range(8):
        routing += jnp.where(ids[:, k : k + 1] == expert_at, shares[:, k : k + 1], 0.0)
    high, low = split_bf16(routing, 2)
    coded = jnp.where(spot < 32, high, low)
    side = (row // 4 == 3 * (1 - odd)) & (lane // 64 == 1 - odd)

    for copy in first:
        copy.wait_recv()

    def part(s):
        return part_send[e] if s == len(PLANE) else part_recv[s]

    lse = [jnp.sum(part(s)[:, 512:].astype(F32), axis=1, keepdims=True) for s in range(16)]
    peak = functools.reduce(jnp.maximum, lse)
    total = jnp.zeros_like(peak)
    summed = jnp.zeros((16, 512), F32)
    for s in range(16):
        weight = jnp.exp2(lse[s] - peak)
        total += weight
        summed += weight * part(s)[:, :512].astype(F32)
    attended = (summed / total).astype(BF16)
    mixed = []
    for h in range(4):
        mapped = jnp.dot(attended, uv[h], preferred_element_type=F32)
        mixed.append(jnp.concatenate([mapped[4 * h : 4 * h + 4]] * 4, axis=0))
    mixed = jnp.concatenate(mixed, axis=1).astype(BF16)

    def terms(to):
        start = pl.multiple_of(window_tile(to) * 128, 128)
        wide = jnp.dot(mixed, outw[:, pl.ds(start, 512)], preferred_element_type=F32)
        folded = wide[:, :128]
        for j in range(1, 4):
            folded = jnp.where(row // 4 == j, wide[:, 128 * j : 128 * j + 128], folded)
        return folded

    second = []
    for k, offset in enumerate(PLANE):
        to = plane_peer(*offset)
        term_send[k] = terms(to).astype(BF16)
        second.append(remote(term_send.at[k], term_recv.at[k], s2.at[k], r2.at[k], {"expert": to}))
        second[-1].start()
    sends += second
    attn_out = terms(e)
    for k, copy in enumerate(second):
        copy.wait_recv()
        attn_out += term_recv[k].astype(F32)

    gains = gain[pl.ds(window_tile(e), 4), :]
    gains = jnp.concatenate([jnp.broadcast_to(gains[j : j + 1], (4, 128)) for j in range(4)], axis=0)
    squares = jnp.sum(jnp.where(side, 0.0, attn_out * attn_out), axis=1, keepdims=True)
    squares = squares[0:4] + squares[4:8] + squares[8:12] + squares[12:16]
    squares = jnp.broadcast_to(jnp.concatenate([squares] * 4, axis=0), (16, 128))
    high, low = split_bf16(squares, 2)
    coded = jnp.where(spot == 0, high, jnp.where(spot == 1, low, coded))
    x_mine[...] = jnp.where(side, coded, attn_out * gains).astype(BF16)
    x_buf[e, core, z] = x_mine[...]
    for k, x, y in OFFSETS:
        to = device(k, x, y)
        if (x, y) == (0, 0):
            copy = remote(x_mine, x_buf.at[e, core, z], s3.at[k - 1], r3.at[z], to)
            sends.append(copy)
        else:
            copy = remote(x_mine, x_buf.at[e, core, z], s4.at[PLANE.index((x, y))], r4.at[e], to)
        copy.start()
    for x, yy in PAIRS:
        for half in range(2):
            source = lax.rem(ex + x, NX) * NX + lax.rem(ey // 2 + yy, 2) * 2 + (odd + half) % 2
            if (x, yy, half) == (0, 0, 0):
                for k in range(1, NX):
                    there = z_peer(k)
                    remote(x_mine, x_buf.at[e, core, there], s3.at[0], r3.at[there], sibling).wait_recv()
            else:
                block = x_buf.at[source, core]
                remote(block, block, s4.at[0], r4.at[source], sibling).wait_recv()
            block = x_buf.at[source, core]
            copy = remote(block, block, s5.at[source], r5.at[source], sibling)
            copy.start()
            sends.append(copy)

    for load in loads[5:]:
        load.wait()
    products = [jnp.zeros((32, 256), F32) for _ in range(2)]
    squares = jnp.zeros((32, 1), F32)
    lane32 = lax.broadcasted_iota(jnp.int32, (32, 128), 1)
    i = lax.broadcasted_iota(jnp.int32, (128, 128), 0)
    j = lax.broadcasted_iota(jnp.int32, (128, 128), 1)
    unfold = (j == (i // 4 % 8) * 16 + (i // 32) * 4 + i % 4).astype(F32).astype(BF16)
    for step, (x, yy) in enumerate(PAIRS):
        pair = lax.rem(ex + x, NX) * 2 + lax.rem(ey // 2 + yy, 2)
        for half in range(2):
            source = pair * 2 + half
            block = x_buf.at[source, 1 - core]
            remote(block, block, s5.at[source], r5.at[source], sibling).wait_recv()
        both = jnp.concatenate([x_buf[pair * 2 + half].reshape(128, 128) for half in range(2)], axis=1)
        both = jnp.dot(unfold, both, preferred_element_type=F32)
        even = [both[32 * n : 32 * n + 32, :128] for n in range(4)]
        odds = [both[32 * n : 32 * n + 32, 128:] for n in range(4)]
        middle = jnp.where(lane32 < 64, even[3], odds[0])
        extra = jnp.where(lane32 < 64, odds[0], even[3])
        squares += jnp.sum(jnp.where(lane32 % 64 < 2, extra, 0.0), axis=1, keepdims=True)
        rows_in = jnp.concatenate(even[:3] + [middle] + odds[1:], axis=1).astype(BF16)
        at = pl.ds(pl.multiple_of(pair * 896, 128), 896)
        for n in range(2):
            weights = jnp.concatenate([gate[n, at, :], up[n, at, :]], axis=1)
            products[n] += jnp.dot(rows_in, weights, preferred_element_type=F32)
        if step == 0:
            share = []
            for n in range(2):
                number = (1 - odd) * 64 + 2 * a + n
                chosen = (lane32 == number + 16) | (lane32 == number + 32)
                share.append(jnp.sum(jnp.where(chosen, extra, 0.0), axis=1, keepdims=True))
    scale = lax.rsqrt(squares / 7168.0 + EPSILON)
    hidden = []
    for n in range(2):
        g = products[n][:, :128] * scale
        u = products[n][:, 128:] * scale
        hidden.append(g / (1.0 + jnp.exp(-g)) * u * share[n])
    hidden = jnp.concatenate(hidden, axis=1).astype(BF16)
    i = lax.broadcasted_iota(jnp.int32, (128, 32), 0)
    j = lax.broadcasted_iota(jnp.int32, (128, 32), 1)
    repeat = (j == i // 16 * 4 + i % 4).astype(F32).astype(BF16)
    hidden = jnp.dot(repeat, hidden, preferred_element_type=F32).astype(BF16)

    row128 = lax.broadcasted_iota(jnp.int32, (128, 128), 0)
    targets = [plane_peer(*offset) for offset in PLANE] + [e]
    swap = []
    for k, to in enumerate(targets):
        start = pl.multiple_of(window_tile(to) * 128, 128)
        wide = jnp.dot(hidden, down[:, pl.ds(start, 512)], preferred_element_type=F32)
        folded = wide[:, :128]
        for j in range(1, 4):
            folded = jnp.where(row128 // 4 % 4 == j, wide[:, 128 * j : 128 * j + 128], folded)
        top, bottom = folded[:64], folded[64:]
        swap_keep[k] = jnp.where(core == 0, top, bottom)
        swap_send[k] = jnp.where(core == 0, bottom, top).astype(BF16)
        swap.append(remote(swap_send.at[k], swap_recv.at[k], s6.at[k], r6.at[k], sibling))
        swap[-1].start()
    sends += swap

    last = []
    for k, to in enumerate(targets):
        swap[k].wait_recv()
        both = swap_keep[k] + swap_recv[k].astype(F32)
        back_send[k] = both.astype(BF16).reshape(NX, 16, 128)
        for n in range(NX):
            there = z_peer(n)
            where = {"attn": there * 2 + core, "expert": to}
            if k < len(PLANE):
                remote(back_send.at[k, there], back_recv.at[k, n], s7.at[k], r7.at[k], where).start()
            elif n > 0:
                last.append(remote(back_send.at[k, there], back_recv.at[k, n], s8.at[n - 1], r8.at[n - 1], where))
                last[-1].start()
    sends += last
    result = attn_out + back_send[len(PLANE), z].astype(F32)
    for n, copy in enumerate(last):
        copy.wait_recv()
        result += back_recv[len(PLANE), n + 1].astype(F32)
    for k in range(len(PLANE)):
        remote(back_recv.at[k], back_recv.at[k], s7.at[k], r7.at[k], sibling).wait_recv()
        for n in range(NX):
            result += back_recv[k, n].astype(F32)
    out_ref[...] = jnp.concatenate([result[4 * j : 4 * j + 4] for j in range(4)], axis=1).astype(BF16)
    for copy in sends:
        copy.wait_send()
    for k in range(len(PLANE)):
        remote(back_send.at[k], back_recv.at[k], s4.at[k], r7.at[k], sibling).wait_send()
        remote(back_send.at[k], back_recv.at[k], s7.at[k], r7.at[k], sibling).wait_send()


def layer(queries, cache, owner, uv, outw, gain, ids, values, gate, up, down):
    dma = pltpu.SemaphoreType.DMA
    hbm = pl.BlockSpec(memory_space=pl.ANY)
    steps = PAGES // STEP_PAGES
    return pl.pallas_call(
        layer_kernel,
        out_shape=jax.ShapeDtypeStruct((4, 512), BF16),
        in_specs=[hbm] * 11,
        out_specs=pl.BlockSpec(memory_space=pltpu.VMEM),
        scratch_shapes=[
            pltpu.SMEM(owner.shape, jnp.int32),
            pltpu.VMEM(queries.shape, BF16),
            pltpu.VMEM((256, 576), BF16),
            pltpu.VMEM(cache.shape, BF16),
            pltpu.VMEM((steps, 256, STEP_PAGES * 64), F32),
            pltpu.VMEM((256, 128), F32),
            pltpu.VMEM((256, 128), F32),
            pltpu.VMEM((256, 512), F32),
            pltpu.VMEM(uv.shape, BF16),
            pltpu.VMEM(outw.shape, BF16),
            pltpu.VMEM(gain.shape, F32),
            pltpu.VMEM(ids.shape, jnp.int32),
            pltpu.VMEM(values.shape, F32),
            pltpu.VMEM(gate.shape, BF16),
            pltpu.VMEM(up.shape, BF16),
            pltpu.VMEM(down.shape, BF16),
            pltpu.VMEM((16, 16, 640), BF16),
            pltpu.VMEM((15, 16, 640), BF16),
            pltpu.VMEM((15, 16, 128), BF16),
            pltpu.VMEM((15, 16, 128), BF16),
            pltpu.VMEM((16, 128), BF16),
            pltpu.VMEM((16, 2, NX, 16, 128), BF16),
            pltpu.VMEM((16, 64, 128), BF16),
            pltpu.VMEM((16, 64, 128), F32),
            pltpu.VMEM((16, 64, 128), BF16),
            pltpu.VMEM((16, NX, 16, 128), BF16),
            pltpu.VMEM((16, NX, 16, 128), BF16),
            dma((10,)), dma((PAGES // LOAD_PAGES,)),
            dma((15,)), dma((15,)),
            dma((15,)), dma((15,)),
            dma((3,)), dma((4,)),
            dma((15,)), dma((16,)),
            dma((16,)), dma((16,)),
            dma((16,)), dma((16,)),
            dma((15,)), dma((15,)),
            dma((3,)), dma((3,)),
        ],
        compiler_params=pltpu.CompilerParams(
            collective_id=0, has_side_effects=True, vmem_limit_bytes=60 << 20
        ),
        name="layer",
    )(queries, cache, owner, uv, outw, gain, ids, values, gate, up, down)


def on_device(
    queries, cache, owner, uv_weight, out_weight, norm_gain, expert_ids, gate_values,
    gate_weight, up_weight, down_weight,
):
    wide = layer(
        queries, cache, owner, uv_weight, out_weight, norm_gain.reshape(56, 128), expert_ids, gate_values,
        gate_weight, up_weight, down_weight.reshape(256, 7168),
    )
    start = (lax.axis_index("expert") % 2) * 64
    return lax.dynamic_slice_in_dim(wide, start, 448, 1)


def solution(mesh):
    placed = (
        P("attn", None, None),
        P(("attn", "expert"), None, None),
        P(("attn", "expert")),
        P("expert", None, None),
        P("expert", None),
        P(),
        P("attn", None),
        P("attn", None),
        P("attn", None, "expert"),
        P("attn", None, "expert"),
        P("attn", "expert", None),
    )
    return jax.shard_map(
        on_device, mesh=mesh, in_specs=placed, out_specs=P("attn", "expert"), check_vma=False
    )
```

```python
import functools
import jax
import jax.numpy as jnp
from jax import lax
from jax.experimental import pallas as pl
from jax.experimental.pallas import tpu as pltpu
from jax.sharding import PartitionSpec as P

SCORE_SCALE = 192.0 ** (-0.5)
LOG2E = 1.4426950408889634
EPSILON = 1e-06
MASKED = -1e30
FLOOR = -1e20
F32 = jnp.float32
BF16 = jnp.bfloat16
MESH = pl.DeviceIdType.MESH

NX = 4
PAGES = 192
STEP_PAGES = 32
LOAD_PAGES = 32
START_WEIGHTS = 0


def hops(steps):
    return sum(min(d, NX - d) for d in steps)


OFFSETS = sorted(
    [(z, x, y) for z in range(NX) for x in range(NX) for y in range(NX) if (z, x, y) != (0, 0, 0)],
    key=lambda d: -hops(d),
)
PLANE = [d[1:] for d in OFFSETS if d[0] == 0]
LAG = 8
AHEAD = 2
PAIRS = [(0, 0), (0, 1), (1, 0), (3, 0), (1, 1), (3, 1), (2, 0), (2, 1)]


def split_bf16(value, parts):
    out = []
    for _ in range(parts):
        piece = value.astype(BF16).astype(F32)
        out.append(piece)
        value = value - piece
    return out


def window_tile(e):
    return (e // 2) * 7 + (e % 2) * 3


def layer_kernel(
    queries_hbm, cache_hbm, owner_hbm, uv_hbm, outw_hbm, gain_hbm, ids_hbm, values_hbm, gate_hbm, up_hbm, down_hbm,
    out_ref,
    owner, queries, q_rows, cache, scores_even, scores_odd, top_even, top_odd, peak_ref, total_ref, value_ref,
    uv, outw, gain, ids_ref, values_ref, gate, up, down,
    part_send, part_recv, term_send, term_recv, x_mine, x_buf,
    swap_send, swap_keep, swap_recv, back_send, back_recv,
    load_sem, cache_sem, s1, r1, s2, r2, s3, r3, s4, r4, s5, r5, s6, r6, s7, r7, s8, r8,
):
    a = lax.axis_index("attn")
    e = lax.axis_index("expert")
    z = a // 2
    core = a % 2
    ex = e // NX
    ey = e % NX
    odd = e % 2
    sibling = {"attn": z * 2 + (1 - core)}

    def plane_peer(x, y):
        return lax.rem(ex + x, NX) * NX + lax.rem(ey + y, NX)

    def z_peer(k):
        return lax.rem(z + k, NX)

    def device(k, x, y):
        return {"attn": z_peer(k) * 2 + core, "expert": plane_peer(x, y)}

    def remote(src, dst, send, recv, to):
        return pltpu.make_async_remote_copy(
            src_ref=src, dst_ref=dst, send_sem=send, recv_sem=recv, device_id=to, device_id_type=MESH
        )

    owner_load = pltpu.make_async_copy(owner_hbm, owner, load_sem.at[0])
    queries_load = pltpu.make_async_copy(queries_hbm, queries, load_sem.at[1])
    owner_load.start()
    queries_load.start()
    cache_loads = []
    for c in range(PAGES // LOAD_PAGES):
        at = pl.ds(c * LOAD_PAGES, LOAD_PAGES)
        cache_loads.append(pltpu.make_async_copy(cache_hbm.at[at], cache.at[at], cache_sem.at[c]))
        cache_loads[-1].start()
    loads = [
        pltpu.make_async_copy(src, dst, load_sem.at[n + 2])
        for n, (src, dst) in enumerate(
            [(uv_hbm, uv), (outw_hbm, outw), (gain_hbm, gain), (ids_hbm, ids_ref), (values_hbm, values_ref),
             (gate_hbm, gate), (up_hbm, up), (down_hbm, down)]
        )
    ]
    barrier = pltpu.get_barrier_semaphore()

    def greet(offsets):
        for offset in offsets:
            pl.semaphore_signal(barrier, inc=1, device_id=device(*offset), device_id_type=MESH)

    pl.semaphore_signal(barrier, inc=1, device_id=sibling, device_id_type=MESH)
    greet(OFFSETS)

    owner_load.wait()
    queries_load.wait()
    rows = 256
    i = lax.broadcasted_iota(jnp.int32, (rows, rows), 0)
    j = lax.broadcasted_iota(jnp.int32, (rows, rows), 1)
    order = (j == (i % 4) * 64 + i // 4).astype(F32).astype(BF16)
    q_rows[...] = jnp.dot(order, queries[...].reshape(rows, 576), preferred_element_type=F32).astype(BF16)
    lane8 = lax.broadcasted_iota(jnp.int32, (8, 128), 1)
    request = lax.broadcasted_iota(jnp.int32, (8, 128), 0) % 4
    tokens = STEP_PAGES * 64
    steps = PAGES // STEP_PAGES
    per = STEP_PAGES // LOAD_PAGES
    peak_ref[...] = jnp.full((rows, 128), FLOOR, F32)
    total_ref[...] = jnp.zeros((rows, 128), F32)
    value_ref[...] = jnp.zeros((rows, 512), F32)
    scores = (scores_even, scores_odd)
    tops = (top_even, top_odd)

    def score(c):
        for load in cache_loads[c * per : (c + 1) * per]:
            load.wait()
        if c == START_WEIGHTS:
            for load in loads:
                load.start()
        keys = cache[c * STEP_PAGES : (c + 1) * STEP_PAGES].reshape(tokens, 576)
        raw = lax.dot_general(q_rows[...], keys, (((1,), (1,)), ((), ())), preferred_element_type=F32)
        top = None
        for pair in range(STEP_PAGES // 2):
            first = owner[c * STEP_PAGES + 2 * pair]
            second = owner[c * STEP_PAGES + 2 * pair + 1]
            bias = jnp.where(jnp.where(lane8 < 64, first, second) == request, 0.0, MASKED)
            tile = raw[:, 128 * pair : 128 * pair + 128].reshape(32, 8, 128) * (SCORE_SCALE * LOG2E) + bias[None]
            tile = tile.reshape(rows, 128)
            scores[c % 2][:, 128 * pair : 128 * pair + 128] = tile
            top = tile if top is None else jnp.maximum(top, tile)
        tops[c % 2][...] = top

    def weigh(c):
        old = peak_ref[...]
        top = jnp.max(tops[c % 2][...], axis=1, keepdims=True)
        peak = jnp.maximum(old, jnp.broadcast_to(top, (rows, 128)))
        alpha = jnp.exp2(old - peak)
        peak_ref[...] = peak
        total = total_ref[...] * alpha
        probs = []
        for pair in range(STEP_PAGES // 2):
            prob = jnp.exp2(scores[c % 2][:, 128 * pair : 128 * pair + 128] - peak)
            total = total + prob
            probs.append(prob.astype(BF16))
        total_ref[...] = total
        values = cache[c * STEP_PAGES : (c + 1) * STEP_PAGES, :, :512].reshape(tokens, 512)
        added = jnp.dot(jnp.concatenate(probs, axis=1), values, preferred_element_type=F32)
        value_ref[...] = value_ref[...] * jnp.concatenate([alpha] * 4, axis=1) + added

    score(0)
    for c in range(steps):
        if c + 1 < steps:
            score(c + 1)
        weigh(c)
    total = jnp.sum(total_ref[...], axis=1, keepdims=True)
    safe = jnp.where(total > 0.0, total, 1.0)
    lse = jnp.where(total > 0.0, peak_ref[...] + jnp.log2(safe), FLOOR)
    wide = lax.broadcasted_iota(jnp.int32, (rows, 128), 1)
    coded = jnp.zeros((rows, 128), F32)
    for at, piece in enumerate(split_bf16(lse, 3)):
        coded = jnp.where(wide == at, piece, coded)
    part_send[:, :, :512] = (value_ref[...] / safe).astype(BF16).reshape(16, 16, 512)
    part_send[:, :, 512:] = coded.astype(BF16).reshape(16, 16, 128)

    pl.semaphore_wait(barrier, len(OFFSETS) + 1)
    sends = []
    for k, offset in enumerate(PLANE):
        to = plane_peer(*offset)
        remote(part_send.at[to], part_recv.at[k], s1, r1, {"expert": to}).start()

    for load in loads[:5]:
        load.wait()
    lane = lax.broadcasted_iota(jnp.int32, (16, 128), 1)
    row = lax.broadcasted_iota(jnp.int32, (16, 128), 0)
    spot = lane % 64
    ids = jnp.concatenate([ids_ref[...]] * 4, axis=0)
    shares = jnp.concatenate([values_ref[...]] * 4, axis=0)
    expert_at = jnp.where(spot < 32, spot - 16, spot - 32)
    expert_at = jnp.where((spot >= 16) & (spot < 48), expert_at, -1)
    routing = jnp.zeros((16, 128), F32)
    for k in range(8):
        routing += jnp.where(ids[:, k : k + 1] == expert_at, shares[:, k : k + 1], 0.0)
    high, low = split_bf16(routing, 2)
    coded = jnp.where(spot < 32, high, low)
    side = (row // 4 == 3 * (1 - odd)) & (lane // 64 == 1 - odd)

    remote(part_recv, part_recv, s1, r1, sibling).wait_recv()

    def part(s):
        return part_send[e] if s == len(PLANE) else part_recv[s]

    lse = [jnp.sum(part(s)[:, 512:].astype(F32), axis=1, keepdims=True) for s in range(16)]
    peak = functools.reduce(jnp.maximum, lse)
    total = jnp.zeros_like(peak)
    summed = jnp.zeros((16, 512), F32)
    for s in range(16):
        weight = jnp.exp2(lse[s] - peak)
        total += weight
        summed += weight * part(s)[:, :512].astype(F32)
    attended = (summed / total).astype(BF16)
    mixed = []
    for h in range(4):
        mapped = jnp.dot(attended, uv[h], preferred_element_type=F32)
        mixed.append(jnp.concatenate([mapped[4 * h : 4 * h + 4]] * 4, axis=0))
    mixed = jnp.concatenate(mixed, axis=1).astype(BF16)

    def terms(to):
        start = pl.multiple_of(window_tile(to) * 128, 128)
        wide = jnp.dot(mixed, outw[:, pl.ds(start, 512)], preferred_element_type=F32)
        folded = wide[:, :128]
        for j in range(1, 4):
            folded = jnp.where(row // 4 == j, wide[:, 128 * j : 128 * j + 128], folded)
        return folded

    for k, offset in enumerate(PLANE):
        to = plane_peer(*offset)
        term_send[k] = terms(to).astype(BF16)
        remote(term_send.at[k], term_recv.at[k], s2, r2, {"expert": to}).start()
    attn_out = terms(e)
    remote(term_recv, term_recv, s2, r2, sibling).wait_recv()
    for k in range(len(PLANE)):
        attn_out += term_recv[k].astype(F32)

    gains = gain[pl.ds(window_tile(e), 4), :]
    gains = jnp.concatenate([jnp.broadcast_to(gains[j : j + 1], (4, 128)) for j in range(4)], axis=0)
    squares = jnp.sum(jnp.where(side, 0.0, attn_out * attn_out), axis=1, keepdims=True)
    squares = squares[0:4] + squares[4:8] + squares[8:12] + squares[12:16]
    squares = jnp.broadcast_to(jnp.concatenate([squares] * 4, axis=0), (16, 128))
    high, low = split_bf16(squares, 2)
    coded = jnp.where(spot == 0, high, jnp.where(spot == 1, low, coded))
    x_mine[...] = jnp.where(side, coded, attn_out * gains).astype(BF16)
    x_buf[e, core, z] = x_mine[...]
    for k, x, y in OFFSETS:
        to = device(k, x, y)
        if (x, y) == (0, 0):
            copy = remote(x_mine, x_buf.at[e, core, z], s3.at[k - 1], r3.at[z], to)
            sends.append(copy)
        else:
            copy = remote(x_mine, x_buf.at[e, core, z], s4, r4.at[e], to)
        copy.start()

    def pass_on(x, yy):
        for half in range(2):
            source = lax.rem(ex + x, NX) * NX + lax.rem(ey // 2 + yy, 2) * 2 + (odd + half) % 2
            if (x, yy, half) == (0, 0, 0):
                for k in range(1, NX):
                    there = z_peer(k)
                    remote(x_mine, x_buf.at[e, core, there], s3.at[0], r3.at[there], sibling).wait_recv()
            else:
                block = x_buf.at[source, core]
                remote(block, block, s4, r4.at[source], sibling).wait_recv()
            block = x_buf.at[source, core]
            remote(block, block, s5, r5.at[source], sibling).start()

    for load in loads[5:]:
        load.wait()
    products = [jnp.zeros((32, 256), F32) for _ in range(2)]
    squares = jnp.zeros((32, 1), F32)
    lane32 = lax.broadcasted_iota(jnp.int32, (32, 128), 1)
    i = lax.broadcasted_iota(jnp.int32, (128, 128), 0)
    j = lax.broadcasted_iota(jnp.int32, (128, 128), 1)
    unfold = (j == (i // 4 % 8) * 16 + (i // 32) * 4 + i % 4).astype(F32).astype(BF16)
    for ahead in PAIRS[:AHEAD]:
        pass_on(*ahead)
    for step, (x, yy) in enumerate(PAIRS):
        if step + AHEAD < len(PAIRS):
            pass_on(*PAIRS[step + AHEAD])
        pair = lax.rem(ex + x, NX) * 2 + lax.rem(ey // 2 + yy, 2)
        for half in range(2):
            source = pair * 2 + half
            block = x_buf.at[source, 1 - core]
            remote(block, block, s5, r5.at[source], sibling).wait_recv()
        both = jnp.concatenate([x_buf[pair * 2 + half].reshape(128, 128) for half in range(2)], axis=1)
        both = jnp.dot(unfold, both, preferred_element_type=F32)
        even = [both[32 * n : 32 * n + 32, :128] for n in range(4)]
        odds = [both[32 * n : 32 * n + 32, 128:] for n in range(4)]
        middle = jnp.where(lane32 < 64, even[3], odds[0])
        extra = jnp.where(lane32 < 64, odds[0], even[3])
        squares += jnp.sum(jnp.where(lane32 % 64 < 2, extra, 0.0), axis=1, keepdims=True)
        rows_in = jnp.concatenate(even[:3] + [middle] + odds[1:], axis=1).astype(BF16)
        at = pl.ds(pl.multiple_of(pair * 896, 128), 896)
        for n in range(2):
            weights = jnp.concatenate([gate[n, at, :], up[n, at, :]], axis=1)
            products[n] += jnp.dot(rows_in, weights, preferred_element_type=F32)
        if step == 0:
            share = []
            for n in range(2):
                number = (1 - odd) * 64 + 2 * a + n
                chosen = (lane32 == number + 16) | (lane32 == number + 32)
                share.append(jnp.sum(jnp.where(chosen, extra, 0.0), axis=1, keepdims=True))
    scale = lax.rsqrt(squares / 7168.0 + EPSILON)
    hidden = []
    for n in range(2):
        g = products[n][:, :128] * scale
        u = products[n][:, 128:] * scale
        hidden.append(g / (1.0 + jnp.exp(-g)) * u * share[n])
    hidden = jnp.concatenate(hidden, axis=1).astype(BF16)
    i = lax.broadcasted_iota(jnp.int32, (128, 32), 0)
    j = lax.broadcasted_iota(jnp.int32, (128, 32), 1)
    repeat = (j == i // 16 * 4 + i % 4).astype(F32).astype(BF16)
    hidden = jnp.dot(repeat, hidden, preferred_element_type=F32).astype(BF16)

    row128 = lax.broadcasted_iota(jnp.int32, (128, 128), 0)
    targets = [plane_peer(*offset) for offset in PLANE] + [e]
    swap = []
    last = []

    def produce(k, to):
        start = pl.multiple_of(window_tile(to) * 128, 128)
        wide = jnp.dot(hidden, down[:, pl.ds(start, 512)], preferred_element_type=F32)
        folded = wide[:, :128]
        for j in range(1, 4):
            folded = jnp.where(row128 // 4 % 4 == j, wide[:, 128 * j : 128 * j + 128], folded)
        top, bottom = folded[:64], folded[64:]
        swap_keep[k] = jnp.where(core == 0, top, bottom)
        swap_send[k] = jnp.where(core == 0, bottom, top).astype(BF16)
        swap.append(remote(swap_send.at[k], swap_recv.at[k], s6, r6.at[k], sibling))
        swap[-1].start()

    def give_back(k, to):
        swap[k].wait_recv()
        both = swap_keep[k] + swap_recv[k].astype(F32)
        back_send[k] = both.astype(BF16).reshape(NX, 16, 128)
        for n in (2, 1, 3, 0):
            there = z_peer(n)
            where = {"attn": there * 2 + core, "expert": to}
            if k < len(PLANE):
                remote(back_send.at[k, there], back_recv.at[k, n], s7, r7, where).start()
            elif n > 0:
                last.append(remote(back_send.at[k, there], back_recv.at[k, n], s8.at[n - 1], r8.at[n - 1], where))
                last[-1].start()

    for k, to in enumerate(targets):
        produce(k, to)
        if k >= LAG:
            give_back(k - LAG, targets[k - LAG])
    for k in range(len(targets) - LAG, len(targets)):
        give_back(k, targets[k])
    sends += last
    result = attn_out + back_send[len(PLANE), z].astype(F32)
    for n in (2, 1, 3):
        remote(x_mine, back_recv.at[len(PLANE), n], s8.at[n - 1], r8.at[n - 1], sibling).wait_recv()
        result += back_recv[len(PLANE), n].astype(F32)
    most = pl.ds(0, len(PLANE))
    remote(back_recv.at[most], back_recv.at[most], s7, r7, sibling).wait_recv()
    for k in range(len(PLANE)):
        for n in range(NX):
            result += back_recv[k, n].astype(F32)
    wide = jnp.concatenate([result[4 * j : 4 * j + 4] for j in range(4)], axis=1)
    out_ref[...] = jnp.where(odd == 1, wide[:, 64:], wide[:, :448]).astype(BF16)
    for copy in sends:
        copy.wait_send()
    remote(part_recv, part_recv, s1, r1, sibling).wait_send()
    remote(term_recv, term_recv, s2, r2, sibling).wait_send()
    remote(back_send.at[most], back_recv.at[most], s4, r7, sibling).wait_send()
    remote(swap_send, swap_recv, s5, r7, sibling).wait_send()
    remote(swap_send, swap_recv, s6, r7, sibling).wait_send()
    remote(back_send.at[most], back_recv.at[most], s7, r7, sibling).wait_send()


def layer(queries, cache, owner, uv, outw, gain, ids, values, gate, up, down):
    dma = pltpu.SemaphoreType.DMA
    hbm = pl.BlockSpec(memory_space=pl.ANY)
    return pl.pallas_call(
        layer_kernel,
        out_shape=jax.ShapeDtypeStruct((4, 448), BF16),
        in_specs=[hbm] * 11,
        out_specs=pl.BlockSpec(memory_space=pltpu.VMEM),
        scratch_shapes=[
            pltpu.SMEM(owner.shape, jnp.int32),
            pltpu.VMEM(queries.shape, BF16),
            pltpu.VMEM((256, 576), BF16),
            pltpu.VMEM(cache.shape, BF16),
            pltpu.VMEM((256, STEP_PAGES * 64), F32),
            pltpu.VMEM((256, STEP_PAGES * 64), F32),
            pltpu.VMEM((256, 128), F32),
            pltpu.VMEM((256, 128), F32),
            pltpu.VMEM((256, 128), F32),
            pltpu.VMEM((256, 128), F32),
            pltpu.VMEM((256, 512), F32),
            pltpu.VMEM(uv.shape, BF16),
            pltpu.VMEM(outw.shape, BF16),
            pltpu.VMEM(gain.shape, F32),
            pltpu.VMEM(ids.shape, jnp.int32),
            pltpu.VMEM(values.shape, F32),
            pltpu.VMEM(gate.shape, BF16),
            pltpu.VMEM(up.shape, BF16),
            pltpu.VMEM(down.shape, BF16),
            pltpu.VMEM((16, 16, 640), BF16),
            pltpu.VMEM((15, 16, 640), BF16),
            pltpu.VMEM((15, 16, 128), BF16),
            pltpu.VMEM((15, 16, 128), BF16),
            pltpu.VMEM((16, 128), BF16),
            pltpu.VMEM((16, 2, NX, 16, 128), BF16),
            pltpu.VMEM((16, 64, 128), BF16),
            pltpu.VMEM((16, 64, 128), F32),
            pltpu.VMEM((16, 64, 128), BF16),
            pltpu.VMEM((16, NX, 16, 128), BF16),
            pltpu.VMEM((16, NX, 16, 128), BF16),
            dma((10,)), dma((PAGES // LOAD_PAGES,)),
            dma, dma,
            dma, dma,
            dma((3,)), dma((4,)),
            dma, dma((16,)),
            dma, dma((16,)),
            dma, dma((16,)),
            dma, dma,
            dma((3,)), dma((3,)),
        ],
        compiler_params=pltpu.CompilerParams(
            collective_id=0, has_side_effects=True, vmem_limit_bytes=60 << 20
        ),
        name="layer",
    )(queries, cache, owner, uv, outw, gain, ids, values, gate, up, down)


def on_device(
    queries, cache, owner, uv_weight, out_weight, norm_gain, expert_ids, gate_values,
    gate_weight, up_weight, down_weight,
):
    return layer(
        queries, cache, owner, uv_weight, out_weight, norm_gain.reshape(56, 128), expert_ids, gate_values,
        gate_weight, up_weight, down_weight.reshape(256, 7168),
    )


def solution(mesh):
    placed = (
        P("attn", None, None),
        P(("attn", "expert"), None, None),
        P(("attn", "expert")),
        P("expert", None, None),
        P("expert", None),
        P(),
        P("attn", None),
        P("attn", None),
        P("attn", None, "expert"),
        P("attn", None, "expert"),
        P("attn", "expert", None),
    )
    return jax.shard_map(
        on_device, mesh=mesh, in_specs=placed, out_specs=P("attn", "expert"), check_vma=False
    )
```

```python
import functools
import jax
import jax.numpy as jnp
from jax import lax
from jax.experimental import pallas as pl
from jax.experimental.pallas import tpu as pltpu
from jax.sharding import PartitionSpec as P

SCORE_SCALE = 192.0 ** (-0.5)
LOG2E = 1.4426950408889634
EPSILON = 1e-06
MASKED = -1e30
FLOOR = -1e20
F32 = jnp.float32
BF16 = jnp.bfloat16
MESH = pl.DeviceIdType.MESH

NX = 4
PAGES = 192
STEP_PAGES = 32


def hops(steps):
    return sum(min(d, NX - d) for d in steps)


OFFSETS = sorted(
    [(z, x, y) for z in range(NX) for x in range(NX) for y in range(NX) if (z, x, y) != (0, 0, 0)],
    key=lambda d: -hops(d),
)
PLANE = [d[1:] for d in OFFSETS if d[0] == 0]
LAG = 8
AHEAD = 2
PAIRS = [(0, 0), (0, 1), (1, 0), (3, 0), (1, 1), (3, 1), (2, 0), (2, 1)]


def split_bf16(value, parts):
    out = []
    for _ in range(parts):
        piece = value.astype(BF16).astype(F32)
        out.append(piece)
        value = value - piece
    return out


def window_tile(e):
    return (e // 2) * 7 + (e % 2) * 3


def attend(owner_hbm, q_hbm, cache_hbm, out_ref, start_weights, owner, q_v, q_rows, cache, sa, sb, ta, tb, m_ref, l_ref, acc_ref, sem, greet):
    CP = STEP_PAGES
    NCH = PAGES // CP
    T = CP * 64
    rows=256
    ld0 = pltpu.make_async_copy(owner_hbm, owner, sem.at[0]); ld0.start()
    ld1 = pltpu.make_async_copy(q_hbm, q_v, sem.at[1]); ld1.start()
    cl = [pltpu.make_async_copy(cache_hbm.at[pl.ds(c*CP,CP)], cache.at[pl.ds(c*CP,CP)], sem.at[2+c]) for c in range(NCH)]
    for c in cl: c.start()
    greet()
    ld0.wait(); ld1.wait()
    i = lax.broadcasted_iota(jnp.int32, (rows, rows), 0)
    j = lax.broadcasted_iota(jnp.int32, (rows, rows), 1)
    order = (j == (i % 4) * 64 + i // 4).astype(F32).astype(BF16)
    q_rows[...] = jnp.dot(order, q_v[...].reshape(rows, 576), preferred_element_type=F32).astype(BF16)
    m_ref[...] = jnp.full_like(m_ref, FLOOR)
    l_ref[...] = jnp.zeros_like(l_ref)
    acc_ref[...] = jnp.zeros_like(acc_ref)
    lane = lax.broadcasted_iota(jnp.int32, (8, 128), 1)
    request = lax.broadcasted_iota(jnp.int32, (8, 128), 0) % 4
    bufs=[sa,sb]; tops=[ta,tb]
    def score(c):
        cl[c].wait()
        if c == 0:
            start_weights()
        keys = cache[c*CP:(c+1)*CP].reshape(T, 576)
        s = lax.dot_general(q_rows[...], keys, (((1,), (1,)), ((), ())), preferred_element_type=F32)
        mx=None
        for pair in range(CP//2):
            first = owner[c * CP + 2 * pair]
            second = owner[c * CP + 2 * pair + 1]
            bias=jnp.where(jnp.where(lane < 64, first, second) == request, 0.0, MASKED)
            t = s[:, 128*pair:128*pair+128].reshape(32,8,128) * (SCORE_SCALE * LOG2E) + bias[None]
            t = t.reshape(256,128)
            bufs[c%2][:, 128*pair:128*pair+128] = t
            mx = t if mx is None else jnp.maximum(mx, t)
        tops[c%2][...] = mx
    def weigh(c):
        old = m_ref[...]
        new = jnp.maximum(old, jnp.broadcast_to(jnp.max(tops[c%2][...],axis=1,keepdims=True),(256,128)))
        alpha = jnp.exp2(old-new)
        m_ref[...] = new
        l = l_ref[...]*alpha
        ps=[]
        for pair in range(T//128):
            p = jnp.exp2(bufs[c%2][:, 128*pair:128*pair+128] - new)
            l = l + p
            ps.append(p.astype(BF16))
        l_ref[...] = l
        vals = cache[c*CP:(c+1)*CP, :, :512].reshape(T, 512)
        d = jnp.dot(jnp.concatenate(ps,axis=1), vals, preferred_element_type=F32)
        acc_ref[...] = acc_ref[...]*jnp.concatenate([alpha]*4,axis=1) + d
    score(0)
    for c in range(NCH):
        if c + 1 < NCH:
            score(c + 1)
        weigh(c)
    total = jnp.sum(l_ref[...], axis=1, keepdims=True)
    safe = jnp.where(total > 0.0, total, 1.0)
    lse = jnp.where(total > 0.0, m_ref[...] + jnp.log2(safe), FLOOR)
    wide = lax.broadcasted_iota(jnp.int32, (256, 128), 1)
    coded = jnp.zeros((256, 128), F32)
    for at, piece in enumerate(split_bf16(lse, 3)):
        coded = jnp.where(wide == at, piece, coded)
    out_ref[:, :, :512] = (acc_ref[...] / safe).astype(BF16).reshape(16, 16, 512)
    out_ref[:, :, 512:] = coded.astype(BF16).reshape(16, 16, 128)


def layer_kernel(
    queries_hbm, cache_hbm, owner_hbm, uv_hbm, outw_hbm, gain_hbm, ids_hbm, values_hbm, gate_hbm, up_hbm, down_hbm,
    out_ref,
    owner, queries, q_rows, cache, scores_even, scores_odd, top_even, top_odd, peak_ref, total_ref, value_ref,
    uv, outw, gain, ids_ref, values_ref, gate, up, down,
    part_send, part_recv, term_send, term_recv, x_mine, x_buf,
    swap_send, swap_keep, swap_recv, back_send, back_recv,
    load_sem, cache_sem, s1, r1, s2, r2, s3, r3, s4, r4, s5, r5, s6, r6, s7, r7, s8, r8,
):
    a = lax.axis_index("attn")
    e = lax.axis_index("expert")
    z = a // 2
    core = a % 2
    ex = e // NX
    ey = e % NX
    odd = e % 2
    sibling = {"attn": z * 2 + (1 - core)}

    def plane_peer(x, y):
        return lax.rem(ex + x, NX) * NX + lax.rem(ey + y, NX)

    def z_peer(k):
        return lax.rem(z + k, NX)

    def device(k, x, y):
        return {"attn": z_peer(k) * 2 + core, "expert": plane_peer(x, y)}

    def remote(src, dst, send, recv, to):
        return pltpu.make_async_remote_copy(
            src_ref=src, dst_ref=dst, send_sem=send, recv_sem=recv, device_id=to, device_id_type=MESH
        )

    loads = [
        pltpu.make_async_copy(src, dst, load_sem.at[n])
        for n, (src, dst) in enumerate(
            [(uv_hbm, uv), (outw_hbm, outw), (gain_hbm, gain), (ids_hbm, ids_ref), (values_hbm, values_ref),
             (gate_hbm, gate), (up_hbm, up), (down_hbm, down)]
        )
    ]
    barrier = pltpu.get_barrier_semaphore()

    def greet():
        pl.semaphore_signal(barrier, inc=1, device_id=sibling, device_id_type=MESH)
        for offset in OFFSETS:
            pl.semaphore_signal(barrier, inc=1, device_id=device(*offset), device_id_type=MESH)

    def start_weights():
        for load in loads:
            load.start()

    attend(
        owner_hbm, queries_hbm, cache_hbm, part_send, start_weights, owner, queries, q_rows, cache,
        scores_even, scores_odd, top_even, top_odd, peak_ref, total_ref, value_ref, cache_sem, greet,
    )

    pl.semaphore_wait(barrier, len(OFFSETS) + 1)
    sends = []
    for k, offset in enumerate(PLANE):
        to = plane_peer(*offset)
        remote(part_send.at[to], part_recv.at[k], s1, r1, {"expert": to}).start()

    for load in loads[:5]:
        load.wait()
    lane = lax.broadcasted_iota(jnp.int32, (16, 128), 1)
    row = lax.broadcasted_iota(jnp.int32, (16, 128), 0)
    spot = lane % 64
    ids = jnp.concatenate([ids_ref[...]] * 4, axis=0)
    shares = jnp.concatenate([values_ref[...]] * 4, axis=0)
    expert_at = jnp.where(spot < 32, spot - 16, spot - 32)
    expert_at = jnp.where((spot >= 16) & (spot < 48), expert_at, -1)
    routing = jnp.zeros((16, 128), F32)
    for k in range(8):
        routing += jnp.where(ids[:, k : k + 1] == expert_at, shares[:, k : k + 1], 0.0)
    high, low = split_bf16(routing, 2)
    coded = jnp.where(spot < 32, high, low)
    side = (row // 4 == 3 * (1 - odd)) & (lane // 64 == 1 - odd)

    remote(part_recv, part_recv, s1, r1, sibling).wait_recv()

    def part(s):
        return part_send[e] if s == len(PLANE) else part_recv[s]

    lse = [jnp.sum(part(s)[:, 512:].astype(F32), axis=1, keepdims=True) for s in range(16)]
    peak = functools.reduce(jnp.maximum, lse)
    total = jnp.zeros_like(peak)
    summed = jnp.zeros((16, 512), F32)
    for s in range(16):
        weight = jnp.exp2(lse[s] - peak)
        total += weight
        summed += weight * part(s)[:, :512].astype(F32)
    attended = (summed / total).astype(BF16)
    mixed = []
    for h in range(4):
        mapped = jnp.dot(attended, uv[h], preferred_element_type=F32)
        mixed.append(jnp.concatenate([mapped[4 * h : 4 * h + 4]] * 4, axis=0))
    mixed = jnp.concatenate(mixed, axis=1).astype(BF16)

    def terms(to):
        start = pl.multiple_of(window_tile(to) * 128, 128)
        wide = jnp.dot(mixed, outw[:, pl.ds(start, 512)], preferred_element_type=F32)
        folded = wide[:, :128]
        for j in range(1, 4):
            folded = jnp.where(row // 4 == j, wide[:, 128 * j : 128 * j + 128], folded)
        return folded

    for k, offset in enumerate(PLANE):
        to = plane_peer(*offset)
        term_send[k] = terms(to).astype(BF16)
        remote(term_send.at[k], term_recv.at[k], s2, r2, {"expert": to}).start()
    attn_out = terms(e)
    remote(term_recv, term_recv, s2, r2, sibling).wait_recv()
    for k in range(len(PLANE)):
        attn_out += term_recv[k].astype(F32)

    gains = gain[pl.ds(window_tile(e), 4), :]
    gains = jnp.concatenate([jnp.broadcast_to(gains[j : j + 1], (4, 128)) for j in range(4)], axis=0)
    squares = jnp.sum(jnp.where(side, 0.0, attn_out * attn_out), axis=1, keepdims=True)
    squares = squares[0:4] + squares[4:8] + squares[8:12] + squares[12:16]
    squares = jnp.broadcast_to(jnp.concatenate([squares] * 4, axis=0), (16, 128))
    high, low = split_bf16(squares, 2)
    coded = jnp.where(spot == 0, high, jnp.where(spot == 1, low, coded))
    x_mine[...] = jnp.where(side, coded, attn_out * gains).astype(BF16)
    x_buf[e, core, z] = x_mine[...]
    for k, x, y in OFFSETS:
        to = device(k, x, y)
        if (x, y) == (0, 0):
            copy = remote(x_mine, x_buf.at[e, core, z], s3.at[k - 1], r3.at[z], to)
            sends.append(copy)
        else:
            copy = remote(x_mine, x_buf.at[e, core, z], s4, r4.at[e], to)
        copy.start()

    def pass_on(x, yy):
        for half in range(2):
            source = lax.rem(ex + x, NX) * NX + lax.rem(ey // 2 + yy, 2) * 2 + (odd + half) % 2
            if (x, yy, half) == (0, 0, 0):
                for k in range(1, NX):
                    there = z_peer(k)
                    remote(x_mine, x_buf.at[e, core, there], s3.at[0], r3.at[there], sibling).wait_recv()
            else:
                block = x_buf.at[source, core]
                remote(block, block, s4, r4.at[source], sibling).wait_recv()
            block = x_buf.at[source, core]
            remote(block, block, s5, r5.at[source], sibling).start()

    for load in loads[5:]:
        load.wait()
    products = [jnp.zeros((32, 256), F32) for _ in range(2)]
    squares = jnp.zeros((32, 1), F32)
    lane32 = lax.broadcasted_iota(jnp.int32, (32, 128), 1)
    i = lax.broadcasted_iota(jnp.int32, (128, 128), 0)
    j = lax.broadcasted_iota(jnp.int32, (128, 128), 1)
    unfold = (j == (i // 4 % 8) * 16 + (i // 32) * 4 + i % 4).astype(F32).astype(BF16)
    for ahead in PAIRS[:AHEAD]:
        pass_on(*ahead)
    for step, (x, yy) in enumerate(PAIRS):
        if step + AHEAD < len(PAIRS):
            pass_on(*PAIRS[step + AHEAD])
        pair = lax.rem(ex + x, NX) * 2 + lax.rem(ey // 2 + yy, 2)
        for half in range(2):
            source = pair * 2 + half
            block = x_buf.at[source, 1 - core]
            remote(block, block, s5, r5.at[source], sibling).wait_recv()
        both = jnp.concatenate([x_buf[pair * 2 + half].reshape(128, 128) for half in range(2)], axis=1)
        both = jnp.dot(unfold, both, preferred_element_type=F32)
        even = [both[32 * n : 32 * n + 32, :128] for n in range(4)]
        odds = [both[32 * n : 32 * n + 32, 128:] for n in range(4)]
        middle = jnp.where(lane32 < 64, even[3], odds[0])
        extra = jnp.where(lane32 < 64, odds[0], even[3])
        squares += jnp.sum(jnp.where(lane32 % 64 < 2, extra, 0.0), axis=1, keepdims=True)
        rows_in = jnp.concatenate(even[:3] + [middle] + odds[1:], axis=1).astype(BF16)
        at = pl.ds(pl.multiple_of(pair * 896, 128), 896)
        for n in range(2):
            weights = jnp.concatenate([gate[n, at, :], up[n, at, :]], axis=1)
            products[n] += jnp.dot(rows_in, weights, preferred_element_type=F32)
        if step == 0:
            share = []
            for n in range(2):
                number = (1 - odd) * 64 + 2 * a + n
                chosen = (lane32 == number + 16) | (lane32 == number + 32)
                share.append(jnp.sum(jnp.where(chosen, extra, 0.0), axis=1, keepdims=True))
    scale = lax.rsqrt(squares / 7168.0 + EPSILON)
    hidden = []
    for n in range(2):
        g = products[n][:, :128] * scale
        u = products[n][:, 128:] * scale
        hidden.append(g / (1.0 + jnp.exp(-g)) * u * share[n])
    hidden = jnp.concatenate(hidden, axis=1).astype(BF16)
    i = lax.broadcasted_iota(jnp.int32, (128, 32), 0)
    j = lax.broadcasted_iota(jnp.int32, (128, 32), 1)
    repeat = (j == i // 16 * 4 + i % 4).astype(F32).astype(BF16)
    hidden = jnp.dot(repeat, hidden, preferred_element_type=F32).astype(BF16)

    row128 = lax.broadcasted_iota(jnp.int32, (128, 128), 0)
    targets = [plane_peer(*offset) for offset in PLANE] + [e]
    swap = []
    last = []

    def produce(k, to):
        start = pl.multiple_of(window_tile(to) * 128, 128)
        wide = jnp.dot(hidden, down[:, pl.ds(start, 512)], preferred_element_type=F32)
        folded = wide[:, :128]
        for j in range(1, 4):
            folded = jnp.where(row128 // 4 % 4 == j, wide[:, 128 * j : 128 * j + 128], folded)
        top, bottom = folded[:64], folded[64:]
        swap_keep[k] = jnp.where(core == 0, top, bottom)
        swap_send[k] = jnp.where(core == 0, bottom, top).astype(BF16)
        swap.append(remote(swap_send.at[k], swap_recv.at[k], s6, r6.at[k], sibling))
        swap[-1].start()

    def give_back(k, to):
        swap[k].wait_recv()
        both = swap_keep[k] + swap_recv[k].astype(F32)
        back_send[k] = both.astype(BF16).reshape(NX, 16, 128)
        for n in (2, 1, 3, 0):
            there = z_peer(n)
            where = {"attn": there * 2 + core, "expert": to}
            if k < len(PLANE):
                remote(back_send.at[k, there], back_recv.at[k, n], s7, r7, where).start()
            elif n > 0:
                last.append(remote(back_send.at[k, there], back_recv.at[k, n], s8.at[n - 1], r8.at[n - 1], where))
                last[-1].start()

    for k, to in enumerate(targets):
        produce(k, to)
        if k >= LAG:
            give_back(k - LAG, targets[k - LAG])
    for k in range(len(targets) - LAG, len(targets)):
        give_back(k, targets[k])
    sends += last
    result = attn_out + back_send[len(PLANE), z].astype(F32)
    for n in (2, 1, 3):
        remote(x_mine, back_recv.at[len(PLANE), n], s8.at[n - 1], r8.at[n - 1], sibling).wait_recv()
        result += back_recv[len(PLANE), n].astype(F32)
    most = pl.ds(0, len(PLANE))
    remote(back_recv.at[most], back_recv.at[most], s7, r7, sibling).wait_recv()
    for k in range(len(PLANE)):
        for n in range(NX):
            result += back_recv[k, n].astype(F32)
    wide = jnp.concatenate([result[4 * j : 4 * j + 4] for j in range(4)], axis=1)
    out_ref[...] = jnp.where(odd == 1, wide[:, 64:], wide[:, :448]).astype(BF16)
    for copy in sends:
        copy.wait_send()
    remote(part_recv, part_recv, s1, r1, sibling).wait_send()
    remote(term_recv, term_recv, s2, r2, sibling).wait_send()
    remote(back_send.at[most], back_recv.at[most], s4, r7, sibling).wait_send()
    remote(swap_send, swap_recv, s5, r7, sibling).wait_send()
    remote(swap_send, swap_recv, s6, r7, sibling).wait_send()
    remote(back_send.at[most], back_recv.at[most], s7, r7, sibling).wait_send()


def layer(queries, cache, owner, uv, outw, gain, ids, values, gate, up, down):
    dma = pltpu.SemaphoreType.DMA
    hbm = pl.BlockSpec(memory_space=pl.ANY)
    return pl.pallas_call(
        layer_kernel,
        out_shape=jax.ShapeDtypeStruct((4, 448), BF16),
        in_specs=[hbm] * 11,
        out_specs=pl.BlockSpec(memory_space=pltpu.VMEM),
        scratch_shapes=[
            pltpu.SMEM(owner.shape, jnp.int32),
            pltpu.VMEM(queries.shape, BF16),
            pltpu.VMEM((256, 576), BF16),
            pltpu.VMEM(cache.shape, BF16),
            pltpu.VMEM((256, STEP_PAGES * 64), F32),
            pltpu.VMEM((256, STEP_PAGES * 64), F32),
            pltpu.VMEM((256, 128), F32),
            pltpu.VMEM((256, 128), F32),
            pltpu.VMEM((256, 128), F32),
            pltpu.VMEM((256, 128), F32),
            pltpu.VMEM((256, 512), F32),
            pltpu.VMEM(uv.shape, BF16),
            pltpu.VMEM(outw.shape, BF16),
            pltpu.VMEM(gain.shape, F32),
            pltpu.VMEM(ids.shape, jnp.int32),
            pltpu.VMEM(values.shape, F32),
            pltpu.VMEM(gate.shape, BF16),
            pltpu.VMEM(up.shape, BF16),
            pltpu.VMEM(down.shape, BF16),
            pltpu.VMEM((16, 16, 640), BF16),
            pltpu.VMEM((15, 16, 640), BF16),
            pltpu.VMEM((15, 16, 128), BF16),
            pltpu.VMEM((15, 16, 128), BF16),
            pltpu.VMEM((16, 128), BF16),
            pltpu.VMEM((16, 2, NX, 16, 128), BF16),
            pltpu.VMEM((16, 64, 128), BF16),
            pltpu.VMEM((16, 64, 128), F32),
            pltpu.VMEM((16, 64, 128), BF16),
            pltpu.VMEM((16, NX, 16, 128), BF16),
            pltpu.VMEM((16, NX, 16, 128), BF16),
            dma((8,)), dma((2 + PAGES // STEP_PAGES,)),
            dma, dma,
            dma, dma,
            dma((3,)), dma((4,)),
            dma, dma((16,)),
            dma, dma((16,)),
            dma, dma((16,)),
            dma, dma,
            dma((3,)), dma((3,)),
        ],
        compiler_params=pltpu.CompilerParams(
            collective_id=0, has_side_effects=True, vmem_limit_bytes=60 << 20
        ),
        name="layer",
    )(queries, cache, owner, uv, outw, gain, ids, values, gate, up, down)


def on_device(
    queries, cache, owner, uv_weight, out_weight, norm_gain, expert_ids, gate_values,
    gate_weight, up_weight, down_weight,
):
    return layer(
        queries, cache, owner, uv_weight, out_weight, norm_gain.reshape(56, 128), expert_ids, gate_values,
        gate_weight, up_weight, down_weight.reshape(256, 7168),
    )


def solution(mesh):
    placed = (
        P("attn", None, None),
        P(("attn", "expert"), None, None),
        P(("attn", "expert")),
        P("expert", None, None),
        P("expert", None),
        P(),
        P("attn", None),
        P("attn", None),
        P("attn", None, "expert"),
        P("attn", None, "expert"),
        P("attn", "expert", None),
    )
    return jax.shard_map(
        on_device, mesh=mesh, in_specs=placed, out_specs=P("attn", "expert"), check_vma=False
    )
```

```python
import functools
import jax
import jax.numpy as jnp
from jax import lax
from jax.experimental import pallas as pl
from jax.experimental.pallas import tpu as pltpu
from jax.sharding import PartitionSpec as P

SCORE_SCALE = 192.0 ** (-0.5)
LOG2E = 1.4426950408889634
EPSILON = 1e-06
MASKED = -1e30
FLOOR = -1e20
F32 = jnp.float32
BF16 = jnp.bfloat16
MESH = pl.DeviceIdType.MESH

NX = 4
PAGES = 192
STEP_PAGES = 32


def hops(steps):
    return sum(min(d, NX - d) for d in steps)


OFFSETS = sorted(
    [(z, x, y) for z in range(NX) for x in range(NX) for y in range(NX) if (z, x, y) != (0, 0, 0)],
    key=lambda d: -hops(d),
)
PLANE = [d[1:] for d in OFFSETS if d[0] == 0]
LAG = 8
AHEAD = 5
PAIRS = [(0, 0), (0, 1), (1, 0), (3, 0), (1, 1), (3, 1), (2, 0), (2, 1)]


def split_bf16(value, parts):
    out = []
    for _ in range(parts):
        piece = value.astype(BF16).astype(F32)
        out.append(piece)
        value = value - piece
    return out


def window_tile(e):
    return (e // 2) * 7 + (e % 2) * 3


def attend(owner_hbm, q_hbm, cache_hbm, out_ref, start_weights, owner, q_v, q_rows, cache, sa, sb, ta, tb, m_ref, l_ref, acc_ref, sem, greet):
    CP = STEP_PAGES
    NCH = PAGES // CP
    T = CP * 64
    rows=256
    ld0 = pltpu.make_async_copy(owner_hbm, owner, sem.at[0]); ld0.start()
    ld1 = pltpu.make_async_copy(q_hbm, q_v, sem.at[1]); ld1.start()
    cl = [pltpu.make_async_copy(cache_hbm.at[pl.ds(c*CP,CP)], cache.at[pl.ds(c*CP,CP)], sem.at[2+c]) for c in range(NCH)]
    for c in cl: c.start()
    greet()
    ld0.wait(); ld1.wait()
    i = lax.broadcasted_iota(jnp.int32, (rows, rows), 0)
    j = lax.broadcasted_iota(jnp.int32, (rows, rows), 1)
    order = (j == (i % 4) * 64 + i // 4).astype(F32).astype(BF16)
    q_rows[...] = jnp.dot(order, q_v[...].reshape(rows, 576), preferred_element_type=F32).astype(BF16)
    m_ref[...] = jnp.full_like(m_ref, FLOOR)
    l_ref[...] = jnp.zeros_like(l_ref)
    acc_ref[...] = jnp.zeros_like(acc_ref)
    lane = lax.broadcasted_iota(jnp.int32, (8, 128), 1)
    request = lax.broadcasted_iota(jnp.int32, (8, 128), 0) % 4
    bufs=[sa,sb]; tops=[ta,tb]
    def score(c):
        cl[c].wait()
        if c == 0:
            start_weights()
        keys = cache[c*CP:(c+1)*CP].reshape(T, 576)
        s = lax.dot_general(q_rows[...], keys, (((1,), (1,)), ((), ())), preferred_element_type=F32)
        mx=None
        for pair in range(CP//2):
            first = owner[c * CP + 2 * pair]
            second = owner[c * CP + 2 * pair + 1]
            bias=jnp.where(jnp.where(lane < 64, first, second) == request, 0.0, MASKED)
            t = s[:, 128*pair:128*pair+128].reshape(32,8,128) * (SCORE_SCALE * LOG2E) + bias[None]
            t = t.reshape(256,128)
            bufs[c%2][:, 128*pair:128*pair+128] = t
            mx = t if mx is None else jnp.maximum(mx, t)
        tops[c%2][...] = mx
    def weigh(c):
        old = m_ref[...]
        new = jnp.maximum(old, jnp.broadcast_to(jnp.max(tops[c%2][...],axis=1,keepdims=True),(256,128)))
        alpha = jnp.exp2(old-new)
        m_ref[...] = new
        l = l_ref[...]*alpha
        ps=[]
        for pair in range(T//128):
            p = jnp.exp2(bufs[c%2][:, 128*pair:128*pair+128] - new)
            l = l + p
            ps.append(p.astype(BF16))
        l_ref[...] = l
        vals = cache[c*CP:(c+1)*CP, :, :512].reshape(T, 512)
        d = jnp.dot(jnp.concatenate(ps,axis=1), vals, preferred_element_type=F32)
        acc_ref[...] = acc_ref[...]*jnp.concatenate([alpha]*4,axis=1) + d
    score(0)
    for c in range(NCH):
        if c + 1 < NCH:
            score(c + 1)
        weigh(c)
    total = jnp.sum(l_ref[...], axis=1, keepdims=True)
    safe = jnp.where(total > 0.0, total, 1.0)
    lse = jnp.where(total > 0.0, m_ref[...] + jnp.log2(safe), FLOOR)
    wide = lax.broadcasted_iota(jnp.int32, (256, 128), 1)
    coded = jnp.zeros((256, 128), F32)
    for at, piece in enumerate(split_bf16(lse, 3)):
        coded = jnp.where(wide == at, piece, coded)
    out_ref[:, :, :512] = (acc_ref[...] / safe).astype(BF16).reshape(16, 16, 512)
    out_ref[:, :, 512:] = coded.astype(BF16).reshape(16, 16, 128)


def layer_kernel(
    queries_hbm, cache_hbm, owner_hbm, uv_hbm, outw_hbm, gain_hbm, ids_hbm, values_hbm, gate_hbm, up_hbm, down_hbm,
    out_ref,
    owner, queries, q_rows, cache, scores_even, scores_odd, top_even, top_odd, peak_ref, total_ref, value_ref,
    uv, outw, gain, ids_ref, values_ref, gate, up, down,
    part_send, part_recv, term_send, term_recv, x_mine, x_buf,
    swap_send, swap_keep, swap_recv, back_send, back_recv,
    load_sem, cache_sem, s1, r1, s2, r2, s3, r3, s4, r4, s5, r5, s6, r6, s7, r7, s8, r8,
):
    a = lax.axis_index("attn")
    e = lax.axis_index("expert")
    z = a // 2
    core = a % 2
    ex = e // NX
    ey = e % NX
    odd = e % 2
    sibling = {"attn": z * 2 + (1 - core)}

    def plane_peer(x, y):
        return lax.rem(ex + x, NX) * NX + lax.rem(ey + y, NX)

    def z_peer(k):
        return lax.rem(z + k, NX)

    def device(k, x, y):
        return {"attn": z_peer(k) * 2 + core, "expert": plane_peer(x, y)}

    def remote(src, dst, send, recv, to):
        return pltpu.make_async_remote_copy(
            src_ref=src, dst_ref=dst, send_sem=send, recv_sem=recv, device_id=to, device_id_type=MESH
        )

    loads = [
        pltpu.make_async_copy(src, dst, load_sem.at[n])
        for n, (src, dst) in enumerate(
            [(uv_hbm, uv), (outw_hbm, outw), (gain_hbm, gain), (ids_hbm, ids_ref), (values_hbm, values_ref),
             (gate_hbm, gate), (up_hbm, up), (down_hbm, down)]
        )
    ]
    barrier = pltpu.get_barrier_semaphore()

    def greet():
        pl.semaphore_signal(barrier, inc=1, device_id=sibling, device_id_type=MESH)
        for offset in OFFSETS:
            pl.semaphore_signal(barrier, inc=1, device_id=device(*offset), device_id_type=MESH)

    def start_weights():
        for load in loads:
            load.start()

    attend(
        owner_hbm, queries_hbm, cache_hbm, part_send, start_weights, owner, queries, q_rows, cache,
        scores_even, scores_odd, top_even, top_odd, peak_ref, total_ref, value_ref, cache_sem, greet,
    )

    pl.semaphore_wait(barrier, len(OFFSETS) + 1)
    sends = []
    for k, offset in enumerate(PLANE):
        to = plane_peer(*offset)
        remote(part_send.at[to], part_recv.at[k], s1, r1, {"expert": to}).start()

    for load in loads[:5]:
        load.wait()
    lane = lax.broadcasted_iota(jnp.int32, (16, 128), 1)
    row = lax.broadcasted_iota(jnp.int32, (16, 128), 0)
    spot = lane % 64
    ids = jnp.concatenate([ids_ref[...]] * 4, axis=0)
    shares = jnp.concatenate([values_ref[...]] * 4, axis=0)
    expert_at = jnp.where(spot < 32, spot - 16, spot - 32)
    expert_at = jnp.where((spot >= 16) & (spot < 48), expert_at, -1)
    routing = jnp.zeros((16, 128), F32)
    for k in range(8):
        routing += jnp.where(ids[:, k : k + 1] == expert_at, shares[:, k : k + 1], 0.0)
    high, low = split_bf16(routing, 2)
    coded = jnp.where(spot < 32, high, low)
    side = (row // 4 == 3 * (1 - odd)) & (lane // 64 == 1 - odd)

    remote(part_recv, part_recv, s1, r1, sibling).wait_recv()

    def part(s):
        return part_send[e] if s == len(PLANE) else part_recv[s]

    lse = [jnp.sum(part(s)[:, 512:].astype(F32), axis=1, keepdims=True) for s in range(16)]
    peak = functools.reduce(jnp.maximum, lse)
    total = jnp.zeros_like(peak)
    summed = jnp.zeros((16, 512), F32)
    for s in range(16):
        weight = jnp.exp2(lse[s] - peak)
        total += weight
        summed += weight * part(s)[:, :512].astype(F32)
    attended = (summed / total).astype(BF16)
    mixed = []
    for h in range(4):
        mapped = jnp.dot(attended, uv[h], preferred_element_type=F32)
        mixed.append(jnp.concatenate([mapped[4 * h : 4 * h + 4]] * 4, axis=0))
    mixed = jnp.concatenate(mixed, axis=1).astype(BF16)

    def terms(to):
        start = pl.multiple_of(window_tile(to) * 128, 128)
        wide = jnp.dot(mixed, outw[:, pl.ds(start, 512)], preferred_element_type=F32)
        folded = wide[:, :128]
        for j in range(1, 4):
            folded = jnp.where(row // 4 == j, wide[:, 128 * j : 128 * j + 128], folded)
        return folded

    for k, offset in enumerate(PLANE):
        to = plane_peer(*offset)
        term_send[k] = terms(to).astype(BF16)
        remote(term_send.at[k], term_recv.at[k], s2, r2, {"expert": to}).start()
    attn_out = terms(e)
    remote(term_recv, term_recv, s2, r2, sibling).wait_recv()
    for k in range(len(PLANE)):
        attn_out += term_recv[k].astype(F32)

    gains = gain[pl.ds(window_tile(e), 4), :]
    gains = jnp.concatenate([jnp.broadcast_to(gains[j : j + 1], (4, 128)) for j in range(4)], axis=0)
    squares = jnp.sum(jnp.where(side, 0.0, attn_out * attn_out), axis=1, keepdims=True)
    squares = squares[0:4] + squares[4:8] + squares[8:12] + squares[12:16]
    squares = jnp.broadcast_to(jnp.concatenate([squares] * 4, axis=0), (16, 128))
    high, low = split_bf16(squares, 2)
    coded = jnp.where(spot == 0, high, jnp.where(spot == 1, low, coded))
    x_mine[...] = jnp.where(side, coded, attn_out * gains).astype(BF16)
    x_buf[e, core, z] = x_mine[...]
    for k, x, y in OFFSETS:
        to = device(k, x, y)
        if (x, y) == (0, 0):
            copy = remote(x_mine, x_buf.at[e, core, z], s3.at[k - 1], r3.at[z], to)
            sends.append(copy)
        else:
            copy = remote(x_mine, x_buf.at[e, core, z], s4, r4.at[e], to)
        copy.start()

    def pass_on(x, yy):
        for half in range(2):
            source = lax.rem(ex + x, NX) * NX + lax.rem(ey // 2 + yy, 2) * 2 + (odd + half) % 2
            if (x, yy, half) == (0, 0, 0):
                for k in range(1, NX):
                    there = z_peer(k)
                    remote(x_mine, x_buf.at[e, core, there], s3.at[0], r3.at[there], sibling).wait_recv()
            else:
                block = x_buf.at[source, core]
                remote(block, block, s4, r4.at[source], sibling).wait_recv()
            block = x_buf.at[source, core]
            remote(block, block, s5, r5.at[source], sibling).start()

    for load in loads[5:]:
        load.wait()
    products = [jnp.zeros((32, 256), F32) for _ in range(2)]
    squares = jnp.zeros((32, 1), F32)
    lane32 = lax.broadcasted_iota(jnp.int32, (32, 128), 1)
    i = lax.broadcasted_iota(jnp.int32, (128, 128), 0)
    j = lax.broadcasted_iota(jnp.int32, (128, 128), 1)
    unfold = (j == (i // 4 % 8) * 16 + (i // 32) * 4 + i % 4).astype(F32).astype(BF16)
    for ahead in PAIRS[:AHEAD]:
        pass_on(*ahead)
    for step, (x, yy) in enumerate(PAIRS):
        if step + AHEAD < len(PAIRS):
            pass_on(*PAIRS[step + AHEAD])
        pair = lax.rem(ex + x, NX) * 2 + lax.rem(ey // 2 + yy, 2)
        for half in range(2):
            source = pair * 2 + half
            block = x_buf.at[source, 1 - core]
            remote(block, block, s5, r5.at[source], sibling).wait_recv()
        both = jnp.concatenate([x_buf[pair * 2 + half].reshape(128, 128) for half in range(2)], axis=1)
        both = jnp.dot(unfold, both, preferred_element_type=F32)
        even = [both[32 * n : 32 * n + 32, :128] for n in range(4)]
        odds = [both[32 * n : 32 * n + 32, 128:] for n in range(4)]
        middle = jnp.where(lane32 < 64, even[3], odds[0])
        extra = jnp.where(lane32 < 64, odds[0], even[3])
        squares += jnp.sum(jnp.where(lane32 % 64 < 2, extra, 0.0), axis=1, keepdims=True)
        rows_in = jnp.concatenate(even[:3] + [middle] + odds[1:], axis=1).astype(BF16)
        at = pl.ds(pl.multiple_of(pair * 896, 128), 896)
        for n in range(2):
            weights = jnp.concatenate([gate[n, at, :], up[n, at, :]], axis=1)
            products[n] += jnp.dot(rows_in, weights, preferred_element_type=F32)
        if step == 0:
            share = []
            for n in range(2):
                number = (1 - odd) * 64 + 2 * a + n
                chosen = (lane32 == number + 16) | (lane32 == number + 32)
                share.append(jnp.sum(jnp.where(chosen, extra, 0.0), axis=1, keepdims=True))
    scale = lax.rsqrt(squares / 7168.0 + EPSILON)
    hidden = []
    for n in range(2):
        g = products[n][:, :128] * scale
        u = products[n][:, 128:] * scale
        hidden.append(g / (1.0 + jnp.exp(-g)) * u * share[n])
    hidden = jnp.concatenate(hidden, axis=1).astype(BF16)
    i = lax.broadcasted_iota(jnp.int32, (128, 32), 0)
    j = lax.broadcasted_iota(jnp.int32, (128, 32), 1)
    repeat = (j == i // 16 * 4 + i % 4).astype(F32).astype(BF16)
    hidden = jnp.dot(repeat, hidden, preferred_element_type=F32).astype(BF16)

    row128 = lax.broadcasted_iota(jnp.int32, (128, 128), 0)
    targets = [plane_peer(*offset) for offset in PLANE] + [e]
    swap = []
    last = []

    def produce(k, to):
        start = pl.multiple_of(window_tile(to) * 128, 128)
        wide = jnp.dot(hidden, down[:, pl.ds(start, 512)], preferred_element_type=F32)
        folded = wide[:, :128]
        for j in range(1, 4):
            folded = jnp.where(row128 // 4 % 4 == j, wide[:, 128 * j : 128 * j + 128], folded)
        top, bottom = folded[:64], folded[64:]
        swap_keep[k] = jnp.where(core == 0, top, bottom)
        swap_send[k] = jnp.where(core == 0, bottom, top).astype(BF16)
        swap.append(remote(swap_send.at[k], swap_recv.at[k], s6, r6.at[k], sibling))
        swap[-1].start()

    def give_back(k, to):
        swap[k].wait_recv()
        both = swap_keep[k] + swap_recv[k].astype(F32)
        back_send[k] = both.astype(BF16).reshape(NX, 16, 128)
        for n in (2, 1, 3, 0):
            there = z_peer(n)
            where = {"attn": there * 2 + core, "expert": to}
            if k < len(PLANE):
                remote(back_send.at[k, there], back_recv.at[k, n], s7, r7, where).start()
            elif n > 0:
                last.append(remote(back_send.at[k, there], back_recv.at[k, n], s8.at[n - 1], r8.at[n - 1], where))
                last[-1].start()

    for k, to in enumerate(targets):
        produce(k, to)
        if k >= LAG:
            give_back(k - LAG, targets[k - LAG])
    for k in range(len(targets) - LAG, len(targets)):
        give_back(k, targets[k])
    sends += last
    result = attn_out + back_send[len(PLANE), z].astype(F32)
    for n in (2, 1, 3):
        remote(x_mine, back_recv.at[len(PLANE), n], s8.at[n - 1], r8.at[n - 1], sibling).wait_recv()
        result += back_recv[len(PLANE), n].astype(F32)
    most = pl.ds(0, len(PLANE))
    remote(back_recv.at[most], back_recv.at[most], s7, r7, sibling).wait_recv()
    for k in range(len(PLANE)):
        for n in range(NX):
            result += back_recv[k, n].astype(F32)
    wide = jnp.concatenate([result[4 * j : 4 * j + 4] for j in range(4)], axis=1)
    out_ref[...] = jnp.where(odd == 1, wide[:, 64:], wide[:, :448]).astype(BF16)
    for copy in sends:
        copy.wait_send()
    remote(part_recv, part_recv, s1, r1, sibling).wait_send()
    remote(term_recv, term_recv, s2, r2, sibling).wait_send()
    remote(back_send.at[most], back_recv.at[most], s4, r7, sibling).wait_send()
    remote(swap_send, swap_recv, s5, r7, sibling).wait_send()
    remote(swap_send, swap_recv, s6, r7, sibling).wait_send()
    remote(back_send.at[most], back_recv.at[most], s7, r7, sibling).wait_send()


def layer(queries, cache, owner, uv, outw, gain, ids, values, gate, up, down):
    dma = pltpu.SemaphoreType.DMA
    hbm = pl.BlockSpec(memory_space=pl.ANY)
    return pl.pallas_call(
        layer_kernel,
        out_shape=jax.ShapeDtypeStruct((4, 448), BF16),
        in_specs=[hbm] * 11,
        out_specs=pl.BlockSpec(memory_space=pltpu.VMEM),
        scratch_shapes=[
            pltpu.SMEM(owner.shape, jnp.int32),
            pltpu.VMEM(queries.shape, BF16),
            pltpu.VMEM((256, 576), BF16),
            pltpu.VMEM(cache.shape, BF16),
            pltpu.VMEM((256, STEP_PAGES * 64), F32),
            pltpu.VMEM((256, STEP_PAGES * 64), F32),
            pltpu.VMEM((256, 128), F32),
            pltpu.VMEM((256, 128), F32),
            pltpu.VMEM((256, 128), F32),
            pltpu.VMEM((256, 128), F32),
            pltpu.VMEM((256, 512), F32),
            pltpu.VMEM(uv.shape, BF16),
            pltpu.VMEM(outw.shape, BF16),
            pltpu.VMEM(gain.shape, F32),
            pltpu.VMEM(ids.shape, jnp.int32),
            pltpu.VMEM(values.shape, F32),
            pltpu.VMEM(gate.shape, BF16),
            pltpu.VMEM(up.shape, BF16),
            pltpu.VMEM(down.shape, BF16),
            pltpu.VMEM((16, 16, 640), BF16),
            pltpu.VMEM((15, 16, 640), BF16),
            pltpu.VMEM((15, 16, 128), BF16),
            pltpu.VMEM((15, 16, 128), BF16),
            pltpu.VMEM((16, 128), BF16),
            pltpu.VMEM((16, 2, NX, 16, 128), BF16),
            pltpu.VMEM((16, 64, 128), BF16),
            pltpu.VMEM((16, 64, 128), F32),
            pltpu.VMEM((16, 64, 128), BF16),
            pltpu.VMEM((16, NX, 16, 128), BF16),
            pltpu.VMEM((16, NX, 16, 128), BF16),
            dma((8,)), dma((2 + PAGES // STEP_PAGES,)),
            dma, dma,
            dma, dma,
            dma((3,)), dma((4,)),
            dma, dma((16,)),
            dma, dma((16,)),
            dma, dma((16,)),
            dma, dma,
            dma((3,)), dma((3,)),
        ],
        compiler_params=pltpu.CompilerParams(
            collective_id=0, has_side_effects=True, vmem_limit_bytes=60 << 20
        ),
        name="layer",
    )(queries, cache, owner, uv, outw, gain, ids, values, gate, up, down)


def on_device(
    queries, cache, owner, uv_weight, out_weight, norm_gain, expert_ids, gate_values,
    gate_weight, up_weight, down_weight,
):
    return layer(
        queries, cache, owner, uv_weight, out_weight, norm_gain.reshape(56, 128), expert_ids, gate_values,
        gate_weight, up_weight, down_weight.reshape(256, 7168),
    )


def solution(mesh):
    placed = (
        P("attn", None, None),
        P(("attn", "expert"), None, None),
        P(("attn", "expert")),
        P("expert", None, None),
        P("expert", None),
        P(),
        P("attn", None),
        P("attn", None),
        P("attn", None, "expert"),
        P("attn", None, "expert"),
        P("attn", "expert", None),
    )
    return jax.shard_map(
        on_device, mesh=mesh, in_specs=placed, out_specs=P("attn", "expert"), check_vma=False
    )
```
